32 devices in a mesh: ctx: 2 (over y), fsdp: 16 (over z, x, core).
Axes of the slice: x: 2, y: 2, z: 4, core: 2. Of those that a mesh axis runs over, the one named last changes fastest.
Arguments:
- tokens: bfloat16 [16, 256, 2048], P('fsdp', 'ctx'), may hold values from -6 to 6
- attn_norm: bfloat16 [2048], P(('ctx', 'fsdp')), may hold values from 0.5 to 1.5
- w_query: bfloat16 [2048, 3072], P(('ctx', 'fsdp')), may hold values from -0.125 to 0.125
- w_latent: bfloat16 [2048, 576], P(('ctx', 'fsdp')), may hold values from -0.125 to 0.125
- latent_norm: bfloat16 [512], P(('ctx', 'fsdp')), may hold values from 0.5 to 1.5
- w_expand: bfloat16 [512, 4096], P(('ctx', 'fsdp')), may hold values from -0.25 to 0.25
- w_output: bfloat16 [2048, 2048], P(('ctx', 'fsdp')), may hold values from -1 to 1
- ffn_norm: bfloat16 [2048], P(('ctx', 'fsdp')), may hold values from 0.5 to 1.5
- w_router: bfloat16 [2048, 16], P(('ctx', 'fsdp')), may hold values from -0.0625 to 0.0625
- shared_gate: bfloat16 [2048, 2816], P(('ctx', 'fsdp')), may hold values from -0.125 to 0.125
- shared_up: bfloat16 [2048, 2816], P(('ctx', 'fsdp')), may hold values from -0.125 to 0.125
- shared_down: bfloat16 [2816, 2048], P(('ctx', 'fsdp')), may hold values from -0.21875 to 0.21875
- expert_gate: bfloat16 [16, 2048, 1408], P('fsdp', 'ctx'), may hold values from -0.125 to 0.125
- expert_up: bfloat16 [16, 2048, 1408], P('fsdp', 'ctx'), may hold values from -0.125 to 0.125
- expert_down: bfloat16 [16, 1408, 2048], P('fsdp', 'ctx'), may hold values from -1.75 to 1.75
- out_grad: bfloat16 [16, 256, 2048], P('fsdp', 'ctx'), may hold values from -6 to 6
- seq_length: int32 [16], P('fsdp'), may hold values from 129 to 256, as said below
- expert_ids: int32 [16, 256, 6], P('fsdp', 'ctx'), may hold values from 0 to 15, all different within a row
- fill_order: int32 [16, 1536], P('fsdp', 'ctx'), may hold values from 0 to 1535, each once within a row
Outputs:
- output: bfloat16 [16, 256, 2048], P('fsdp', 'ctx')
- input_grad: bfloat16 [16, 256, 2048], P('fsdp', 'ctx')
- attn_norm_grad: float32 [2048], P(('ctx', 'fsdp'))
- w_query_grad: float32 [2048, 3072], P(('ctx', 'fsdp'))
- w_latent_grad: float32 [2048, 576], P(('ctx', 'fsdp'))
- latent_norm_grad: float32 [512], P(('ctx', 'fsdp'))
- w_expand_grad: float32 [512, 4096], P(('ctx', 'fsdp'))
- w_output_grad: float32 [2048, 2048], P(('ctx', 'fsdp'))
- ffn_norm_grad: float32 [2048], P(('ctx', 'fsdp'))
- w_router_grad: float32 [2048, 16], P(('ctx', 'fsdp'))
- shared_gate_grad: float32 [2048, 2816], P(('ctx', 'fsdp'))
- shared_up_grad: float32 [2048, 2816], P(('ctx', 'fsdp'))
- shared_down_grad: float32 [2816, 2048], P(('ctx', 'fsdp'))
- expert_gate_grad: float32 [16, 2048, 1408], P('fsdp', 'ctx')
- expert_up_grad: float32 [16, 2048, 1408], P('fsdp', 'ctx')
- expert_down_grad: float32 [16, 1408, 2048], P('fsdp', 'ctx')
The draws below stay inside these ranges and needn't reach their ends.
Inputs may be any that keep to these rules, and one draw needn't show every extreme that they name: `seq_length`: every sequence ends on its last device's block; some sequence uses all 256 positions. `expert_ids`: each token names 6 different experts. `fill_order`: each sequence's entries are all different.
All inputs are finite; a program needn't handle non-finite values.
Results may differ from the reference program's by a relative error of at most 0.02.
Values may be sent and summed in bfloat16 or wider, within the bound.
No kernel may reach another device: no remote copies, remote signals or barrier semaphores. Data moves between devices by JAX's collectives and lax.ppermute only.
A program may use at most 384 MiB of HBM per device.

```python
import jax
import jax.numpy as jnp
from jax import lax

MODEL_WIDTH = 2048
HEADS = 16
NOPE = 128
ROPE = 64
VDIM = 128
KVR = 512
FF = 1408
SHARED = 2816
TOPK = 6
TOK_DEV = 128
EXPERTS = 16
SEQS = 16
SEQLEN = 256
CAP = 48
N_CTX = 2


def draw_seq_length(key, part):
    key = jax.random.fold_in(key, 3)
    first_key, second_key = jax.random.split(key)
    drawn = jax.random.randint(first_key, (SEQS,), SEQLEN - TOK_DEV + 1, SEQLEN + 1)
    picked = jax.random.randint(second_key, (), 0, SEQS)
    return jnp.where(jnp.arange(SEQS) == picked, SEQLEN, drawn).astype(jnp.int32)


def levels(stream_key, extent, pieces, least, largest):
    factor_of, own = 1.0, jax.random.fold_in(stream_key, 6)
    for axis_at, blocks in pieces:
        draws = jnp.exp(jax.random.uniform(jax.random.fold_in(own, axis_at), (blocks,), jnp.float32, least / len(pieces), largest / len(pieces)))
        factor_of = factor_of * jnp.repeat(draws, extent[axis_at] // blocks).reshape([-1 if axis == axis_at else 1 for axis in range(len(extent))])
    return factor_of


def different_ones(key, rows, amount, top, lift):
    order = jax.random.permutation(jax.random.fold_in(key, 1), amount)
    boost = order
    for power in range(3):
        boost = boost * boost // amount
    boost = boost * lift // amount
    tickets = jax.random.randint(jax.random.fold_in(key, 2), (rows, amount), 0, 4096) + boost
    sure = jax.random.permutation(jax.random.fold_in(key, 3), rows)[jnp.arange(amount) % rows]
    tickets = jnp.where(jnp.arange(rows)[:, None] == sure[None, :], 1 << 14, tickets)
    merit = tickets * amount + jnp.arange(amount)
    return lax.top_k(merit.astype(jnp.int32), top)[1].astype(jnp.int32)


def bell_draw(key, extent, deviation, most, cuts=(), kind=jnp.bfloat16):
    values = deviation * jax.random.normal(key, extent, jnp.float32)
    if cuts:
        values = values * levels(key, extent, cuts, -0.22, 0.18)
    return jnp.clip(values, -most, most).astype(kind)


def setup_inputs(seed: int = 0) -> dict:
    streams_of = jax.random.split(jax.random.key(seed), 20)
    return {
        "tokens": bell_draw(streams_of[0], (SEQS, SEQLEN, MODEL_WIDTH), 1.0, 6.0, ((0, 16), (1, 2))),
        "attn_norm": jnp.clip(1.0 + 0.1 * jax.random.normal(streams_of[1], (MODEL_WIDTH,), jnp.float32), 0.5, 1.5).astype(jnp.bfloat16),
        "w_query": bell_draw(streams_of[2], (MODEL_WIDTH, HEADS * (NOPE + ROPE)), MODEL_WIDTH ** -0.5, 0.125, ((0, 32),)),
        "w_latent": bell_draw(streams_of[3], (MODEL_WIDTH, KVR + ROPE), MODEL_WIDTH ** -0.5, 0.125, ((0, 32),)),
        "latent_norm": jnp.clip(1.0 + 0.1 * jax.random.normal(streams_of[4], (KVR,), jnp.float32), 0.5, 1.5).astype(jnp.bfloat16),
        "w_expand": bell_draw(streams_of[5], (KVR, HEADS * (NOPE + VDIM)), KVR ** -0.5, 0.25, ((0, 32),)),
        "w_output": bell_draw(streams_of[6], (HEADS * VDIM, MODEL_WIDTH), (max(HEADS * VDIM // 64, 1)) ** -0.5, 1.0, ((0, 32),)),
        "ffn_norm": jnp.clip(1.0 + 0.1 * jax.random.normal(streams_of[7], (MODEL_WIDTH,), jnp.float32), 0.5, 1.5).astype(jnp.bfloat16),
        "w_router": bell_draw(streams_of[8], (MODEL_WIDTH, EXPERTS), (4 * MODEL_WIDTH) ** -0.5, 0.0625, ((0, 32),)),
        "shared_gate": bell_draw(streams_of[9], (MODEL_WIDTH, SHARED), MODEL_WIDTH ** -0.5, 0.125, ((0, 32),)),
        "shared_up": bell_draw(streams_of[10], (MODEL_WIDTH, SHARED), MODEL_WIDTH ** -0.5, 0.125, ((0, 32),)),
        "shared_down": bell_draw(streams_of[11], (SHARED, MODEL_WIDTH), (max(SHARED // 4, 1)) ** -0.5, 0.21875, ((0, 32),)),
        "expert_gate": bell_draw(streams_of[12], (EXPERTS, MODEL_WIDTH, FF), MODEL_WIDTH ** -0.5, 0.125, ((0, 16), (1, 2))),
        "expert_up": bell_draw(streams_of[13], (EXPERTS, MODEL_WIDTH, FF), MODEL_WIDTH ** -0.5, 0.125, ((0, 16), (1, 2))),
        "expert_down": bell_draw(streams_of[14], (EXPERTS, FF, MODEL_WIDTH), (max(FF // 128, 1)) ** -0.5, 1.75, ((0, 16), (1, 2))),
        "out_grad": bell_draw(streams_of[15], (SEQS, SEQLEN, MODEL_WIDTH), 1.0, 6.0, ((0, 16), (1, 2))),
        "seq_length": draw_seq_length(jax.random.fold_in(streams_of[19], 71), 0),
        "expert_ids": different_ones(streams_of[17], SEQS * SEQLEN, EXPERTS, TOPK, 3072).reshape((SEQS, SEQLEN, TOPK)),
        "fill_order": jax.vmap(lambda own: jax.random.permutation(own, SEQLEN * TOPK))(jax.random.split(streams_of[18], SEQS)).reshape((SEQS, SEQLEN * TOPK)).astype(jnp.int32),
    }


@jax.custom_vjp
def low(v):
    return lax.optimization_barrier(v.astype(jnp.bfloat16)).astype(jnp.float32)

@jax.custom_vjp
def low_back(v):
    return v

def low_keep(v):
    return (low(v), None)

def low_pass(kept, grad):
    return (grad,)

def back_keep(v):
    return (v, None)

def back_low(kept, grad):
    return (low(grad),)
low.defvjp(low_keep, low_pass)
low_back.defvjp(back_keep, back_low)
EPSILON = 1e-06
ROPE_BASE = 10000.0
NEGATIVE_FILL = -1e+30

def highest(left, right):
    return jnp.dot(left, right, precision=lax.Precision.HIGHEST)

def rms_norm(values, gain):
    return values * lax.rsqrt(lax.optimization_barrier(jnp.mean(values * values, axis=-1, keepdims=True)) + EPSILON) * gain

def rope_tables(positions, width):
    half = width // 2
    freqs = ROPE_BASE ** (-jnp.arange(half, dtype=jnp.float32) / half)
    angles = positions.astype(jnp.float32)[:, None] * freqs[None, :]
    return (jnp.cos(angles), jnp.sin(angles))

def rotate(values, cosine, sine):
    half = values.shape[-1] // 2
    first = values[..., :half]
    second = values[..., half:]
    return jnp.concatenate([first * cosine - second * sine, second * cosine + first * sine], axis=-1)

def slot_rank(expert_flat, priority):
    same = (expert_flat[:, None] == expert_flat[None, :]) & (priority[None, :] < priority[:, None])
    return lax.optimization_barrier(jnp.sum(same.astype(jnp.int32), axis=1)).astype(jnp.int32)

def attend(items):
    queries, key_nope, values, key_rope, length = items
    span = queries.shape[0]
    block_count = span // TOK_DEV
    query_blocks = queries.reshape(block_count, TOK_DEV, HEADS, NOPE + ROPE)
    starts = jnp.arange(block_count, dtype=jnp.int32) * TOK_DEV
    key_index = jnp.arange(span, dtype=jnp.int32)

    def query_block(block_items):
        block_queries, start = block_items
        nope_block = low_back(key_nope)
        value_block = low_back(values)
        keys = jnp.concatenate([nope_block, jnp.broadcast_to(key_rope[:, None, :], (span, HEADS, ROPE))], axis=-1)
        scores = jnp.einsum('ihd,jhd->hij', block_queries, keys, precision=lax.Precision.HIGHEST)
        scores = low_back(scores * (NOPE + ROPE) ** (-0.5))
        query_index = start + jnp.arange(TOK_DEV, dtype=jnp.int32)
        allowed = (key_index[None, :] <= query_index[:, None]) & (key_index[None, :] < length)
        scores = jnp.where(allowed[None], scores, NEGATIVE_FILL)
        probs = jax.nn.softmax(scores, axis=-1)
        attended = jnp.einsum('hij,jhd->ihd', low(probs), value_block, precision=lax.Precision.HIGHEST)
        return low(low_back(attended))
    result = lax.map(jax.checkpoint(query_block), (query_blocks, starts))
    return result.reshape(span, HEADS, VDIM)

def apply_expert_layer(items):
    token_rows, w_gate, w_up, w_down = items
    gate_val = low_back(highest(token_rows, w_gate))
    up_val = low_back(highest(token_rows, w_up))
    active = low(jax.nn.silu(gate_val) * up_val)
    return low(low_back(highest(active, w_down)))

def reference(tokens, attn_norm, w_query, w_latent, latent_norm, w_expand, w_output, ffn_norm, w_router, shared_gate, shared_up, shared_down, expert_gate, expert_up, expert_down, out_grad, seq_length, expert_ids, fill_order):
    tok_all = SEQS * SEQLEN
    n_blocks = SEQS * N_CTX
    expert_slots = EXPERTS * n_blocks * CAP
    positions = jnp.tile(jnp.arange(SEQLEN, dtype=jnp.int32), SEQS)
    cosine, sine = rope_tables(positions, ROPE)
    valid = (jnp.arange(SEQLEN)[None, :] < seq_length[:, None]).reshape(tok_all).astype(jnp.float32)
    block_ids = expert_ids.reshape(n_blocks, TOK_DEV * TOPK).astype(jnp.int32)
    block_prio = fill_order.reshape(n_blocks, TOK_DEV * TOPK).astype(jnp.int32)
    ranks = lax.map(lambda pair: slot_rank(pair[0], pair[1]), (block_ids, block_prio))
    kept = ranks < CAP
    block_index = jnp.arange(n_blocks, dtype=jnp.int32)[:, None]
    dest = jnp.where(kept, block_ids * (n_blocks * CAP) + block_index * CAP + ranks, expert_slots).reshape(-1).astype(jnp.int32)
    pair_token = (jnp.arange(tok_all * TOPK) // TOPK).astype(jnp.int32)
    kept_pairs = kept.reshape(tok_all, TOPK).astype(jnp.float32)
    onehot = (expert_ids.reshape(tok_all, TOPK)[:, :, None] == jnp.arange(EXPERTS)[None, None, :]).astype(jnp.float32)

    def layer_forward(input_rows, attention_gain, query_weight, latent_down_weight, latent_gain, latent_up_weight, output_weight, feedforward_gain, router_weight, shared_gate_weight, shared_up_weight, shared_down_weight, expert_gate_weight, expert_up_weight, expert_down_weight):
        h_attn = low(rms_norm(input_rows, attention_gain))
        query_raw = low_back(highest(h_attn, query_weight)).reshape(tok_all, HEADS, NOPE + ROPE)
        query_rot = low(jnp.concatenate([query_raw[..., :NOPE], rotate(query_raw[..., NOPE:], cosine[:, None, :], sine[:, None, :])], axis=-1))
        latent_in = low_back(highest(h_attn, latent_down_weight))
        latent = low(rms_norm(latent_in[:, :KVR], latent_gain))
        key_rope = low(rotate(latent_in[:, KVR:], cosine, sine))
        expanded = highest(latent, latent_up_weight).reshape(tok_all, HEADS, NOPE + VDIM)
        key_nope = low(expanded[..., :NOPE])
        values = low(expanded[..., NOPE:])
        attended = lax.map(jax.checkpoint(attend), (query_rot.reshape(SEQS, SEQLEN, HEADS, NOPE + ROPE), key_nope.reshape(SEQS, SEQLEN, HEADS, NOPE), values.reshape(SEQS, SEQLEN, HEADS, VDIM), key_rope.reshape(SEQS, SEQLEN, ROPE), seq_length))
        attn_out = low_back(highest(attended.reshape(tok_all, HEADS * VDIM), output_weight))
        middle = input_rows + attn_out
        h_ffn = low(rms_norm(middle, feedforward_gain))
        gates = jax.nn.softmax(highest(h_ffn, router_weight), axis=-1)
        chosen = jnp.einsum('tke,te->tk', onehot, gates, precision=lax.Precision.HIGHEST)
        shared_gate_val = low_back(highest(h_ffn, shared_gate_weight))
        shared_up_val = low_back(highest(h_ffn, shared_up_weight))
        shared_act = low(jax.nn.silu(shared_gate_val) * shared_up_val)
        shared_out = low_back(highest(shared_act, shared_down_weight))
        slot_buffer = jnp.zeros((expert_slots + 1, MODEL_WIDTH), jnp.float32).at[dest].set(h_ffn[pair_token])[:expert_slots]
        slot_buffer = low_back(slot_buffer).reshape(EXPERTS, n_blocks * CAP, MODEL_WIDTH)
        expert_output = lax.map(jax.checkpoint(apply_expert_layer), (slot_buffer, expert_gate_weight, expert_up_weight, expert_down_weight)).reshape(expert_slots, MODEL_WIDTH)
        pair_out = jnp.concatenate([expert_output, jnp.zeros((1, MODEL_WIDTH), jnp.float32)], axis=0)[dest].reshape(tok_all, TOPK, MODEL_WIDTH)
        routed = jnp.einsum('tk,tkd->td', chosen * kept_pairs, pair_out, precision=lax.Precision.HIGHEST)
        return middle + shared_out + routed
    primals = tuple((arr.astype(jnp.float32) for arr in (tokens.reshape(tok_all, MODEL_WIDTH), attn_norm, w_query, w_latent, latent_norm, w_expand, w_output, ffn_norm, w_router, shared_gate, shared_up, shared_down, expert_gate, expert_up, expert_down)))
    result, pullback = jax.vjp(layer_forward, *primals)
    grads = pullback(out_grad.reshape(tok_all, MODEL_WIDTH).astype(jnp.float32) * valid[:, None])
    return (result.astype(jnp.bfloat16).reshape(SEQS, SEQLEN, MODEL_WIDTH), grads[0].astype(jnp.bfloat16).reshape(SEQS, SEQLEN, MODEL_WIDTH), grads[1], grads[2], grads[3], grads[4], grads[5], grads[6], grads[7], grads[8], grads[9], grads[10], grads[11], grads[12], grads[13], grads[14])
```

```python
import jax
import jax.numpy as jnp
from jax import lax
from jax.experimental import pallas as pl
from jax.experimental.pallas import tpu as pltpu
from jax.sharding import Mesh
from jax.sharding import PartitionSpec as P

HEADS = 16
NOPE = 128
ROPE = 64
VDIM = 128
KVR = 512
TOPK = 6


EPSILON = 1e-06
ROPE_BASE = 10000.0
NEGATIVE_FILL = -1e30


def matrix_product(left, right):
    return jnp.dot(left, right, preferred_element_type=jnp.float32)


def rms_norm(values, gain):
    return values * lax.rsqrt(jnp.mean(values * values, axis=-1, keepdims=True) + EPSILON) * gain


def norm_back(values, gain, grad_out):
    inverse = lax.rsqrt(jnp.mean(values * values, axis=-1, keepdims=True) + EPSILON)
    normed = values * inverse
    gain_grad = jnp.sum(grad_out * normed, axis=0)
    scaled = grad_out * gain
    input_grad = inverse * (scaled - normed * jnp.mean(scaled * normed, axis=-1, keepdims=True))
    return (input_grad, gain_grad)


def rope_tables(positions, width):
    half = width // 2
    freqs = ROPE_BASE ** (-jnp.arange(half, dtype=jnp.float32) / half)
    angles = positions.astype(jnp.float32)[:, None] * freqs[None, :]
    return (jnp.cos(angles), jnp.sin(angles))


def rotate(values, cosine, sine):
    half = values.shape[-1] // 2
    first = values[..., :half]
    second = values[..., half:]
    return jnp.concatenate(
        [first * cosine - second * sine, second * cosine + first * sine], axis=-1
    )


def rotate_back(grads, cosine, sine):
    half = grads.shape[-1] // 2
    first = grads[..., :half]
    second = grads[..., half:]
    return jnp.concatenate(
        [first * cosine + second * sine, second * cosine - first * sine], axis=-1
    )


def slot_rank(expert_flat, priority):
    same = (expert_flat[:, None] == expert_flat[None, :]) & (priority[None, :] < priority[:, None])
    return jnp.sum(same.astype(jnp.int32), axis=1)


def swish_gradients(d_act, gate_val, up_val):
    sigma = jax.nn.sigmoid(gate_val)
    d_gate = (d_act * up_val * sigma * (1.0 + gate_val * (1.0 - sigma))).astype(jnp.bfloat16)
    d_up = (d_act * gate_val * sigma).astype(jnp.bfloat16)
    return (d_gate, d_up)


def local_weights(
    tokens,
    attn_norm,
    w_query,
    w_latent,
    latent_norm,
    w_expand,
    w_output,
    ffn_norm,
    w_router,
    shared_gate,
    shared_up,
    shared_down,
    expert_gate,
    expert_up,
    expert_down,
    out_grad,
    seq_length,
    expert_ids,
    fill_order,
):
    input_rows = tokens[0].astype(jnp.float32)
    tok_count = input_rows.shape[0]
    width = input_rows.shape[1]
    n_experts = expert_gate.shape[0] * lax.axis_size("fsdp")
    capacity = tok_count * TOPK // n_experts
    pair_count = tok_count * TOPK
    softmax_scale = (NOPE + ROPE) ** (-0.5)
    positions = lax.axis_index("ctx") * tok_count + jnp.arange(tok_count, dtype=jnp.int32)
    seq_used = seq_length[0]
    valid = (positions < seq_used).astype(jnp.float32)
    cosine, sine = rope_tables(positions, ROPE)
    attention_gain, wq_full, wkva_full, latent_gain, wkvb_full, wo_full = (
        lax.all_gather(attn_norm, ("ctx", "fsdp"), axis=0, tiled=True),
        lax.all_gather(w_query, ("ctx", "fsdp"), axis=0, tiled=True),
        lax.all_gather(w_latent, ("ctx", "fsdp"), axis=0, tiled=True),
        lax.all_gather(latent_norm, ("ctx", "fsdp"), axis=0, tiled=True),
        lax.all_gather(w_expand, ("ctx", "fsdp"), axis=0, tiled=True),
        lax.all_gather(w_output, ("ctx", "fsdp"), axis=0, tiled=True),
    )
    attention_gain = attention_gain.astype(jnp.float32)
    latent_gain = latent_gain.astype(jnp.float32)
    h_attn = rms_norm(input_rows, attention_gain).astype(jnp.bfloat16)
    query_raw = matrix_product(h_attn, wq_full).reshape(tok_count, HEADS, NOPE + ROPE)
    query_rot = jnp.concatenate(
        [
            query_raw[..., :NOPE],
            rotate(query_raw[..., NOPE:], cosine[:, None, :], sine[:, None, :]),
        ],
        axis=-1,
    ).astype(jnp.bfloat16)
    latent_in = matrix_product(h_attn, wkva_full)
    latent_raw = latent_in[:, :KVR]
    latent = rms_norm(latent_raw, latent_gain).astype(jnp.bfloat16)
    key_rope = rotate(latent_in[:, KVR:], cosine, sine).astype(jnp.bfloat16)
    latent_all, rope_all = (
        lax.all_gather(latent, "ctx", axis=0, tiled=True),
        lax.all_gather(key_rope, "ctx", axis=0, tiled=True),
    )
    expand_all = matrix_product(latent_all, wkvb_full).astype(jnp.bfloat16)
    seq_total = expand_all.shape[0]
    expand_heads = jnp.transpose(expand_all.reshape(seq_total, HEADS, NOPE + VDIM), (1, 0, 2))
    nope_heads = expand_heads[..., :NOPE]
    value_heads = expand_heads[..., NOPE:]
    query_heads = jnp.transpose(query_rot, (1, 0, 2))
    key_pos = jnp.arange(seq_total, dtype=jnp.int32)
    allowed = (key_pos[None, :] <= positions[:, None]) & (key_pos[None, :] < seq_used)

    def head_scores(query_h, nope_h):
        keys = jnp.concatenate([nope_h, rope_all], axis=-1)
        scores = matrix_product(query_h, keys.T) * softmax_scale
        return (jnp.where(allowed, scores, NEGATIVE_FILL), keys)

    def head_forward(items):
        query_h, nope_h, value_h = items
        scores, keys = head_scores(query_h, nope_h)
        highest_score = jnp.max(scores, axis=-1, keepdims=True)
        expo = jnp.exp(scores - highest_score)
        total = jnp.sum(expo, axis=-1, keepdims=True)
        probs = (expo / total).astype(jnp.bfloat16)
        attended_h = matrix_product(probs, value_h).astype(jnp.bfloat16)
        return (attended_h, highest_score[:, 0] + jnp.log(total[:, 0]))

    attended_heads, lse_heads = lax.map(head_forward, (query_heads, nope_heads, value_heads))
    attended = jnp.transpose(attended_heads, (1, 0, 2)).reshape(tok_count, HEADS * VDIM)
    middle = input_rows + matrix_product(attended, wo_full)
    feedforward_gain, router_full, sgate_full, sup_full, sdown_full = (
        lax.all_gather(ffn_norm, ("ctx", "fsdp"), axis=0, tiled=True),
        lax.all_gather(w_router, ("ctx", "fsdp"), axis=0, tiled=True),
        lax.all_gather(shared_gate, ("ctx", "fsdp"), axis=0, tiled=True),
        lax.all_gather(shared_up, ("ctx", "fsdp"), axis=0, tiled=True),
        lax.all_gather(shared_down, ("ctx", "fsdp"), axis=0, tiled=True),
    )
    feedforward_gain = feedforward_gain.astype(jnp.float32)
    expert_gate_gathered, expert_up_gathered, expert_down_gathered = (
        lax.all_gather(expert_gate, "ctx", axis=1, tiled=True),
        lax.all_gather(expert_up, "ctx", axis=1, tiled=True),
        lax.all_gather(expert_down, "ctx", axis=1, tiled=True),
    )
    expert_gate_matrix = expert_gate_gathered[0]
    expert_up_matrix = expert_up_gathered[0]
    edown_w = expert_down_gathered[0]
    h_ffn = rms_norm(middle, feedforward_gain).astype(jnp.bfloat16)
    gates = jax.nn.softmax(matrix_product(h_ffn, router_full), axis=-1)
    route_ids = expert_ids[0]
    onehot = (
        route_ids[:, :, None] == jnp.arange(n_experts, dtype=jnp.int32)[None, None, :]
    ).astype(jnp.float32)
    chosen = jnp.einsum("tke,te->tk", onehot, gates, precision=lax.Precision.HIGHEST)
    shared_gate_val = matrix_product(h_ffn, sgate_full)
    shared_up_val = matrix_product(h_ffn, sup_full)
    shared_act = (jax.nn.silu(shared_gate_val) * shared_up_val).astype(jnp.bfloat16)
    shared_out = matrix_product(shared_act, sdown_full)
    flat_ids = route_ids.reshape(pair_count)
    ranks = slot_rank(flat_ids, fill_order[0])
    kept = ranks < capacity
    dest = jnp.where(kept, flat_ids * capacity + ranks, n_experts * capacity)
    pair_token = jnp.arange(pair_count) // TOPK
    slot_total = n_experts * capacity
    send_rows = (
        jnp.zeros((slot_total + 1, width), jnp.bfloat16)
        .at[dest]
        .set(h_ffn[pair_token])[:slot_total]
    )
    received = lax.all_to_all(
        send_rows.reshape(n_experts, capacity, width),
        "fsdp",
        split_axis=0,
        concat_axis=0,
        tiled=True,
    )
    token_rows = received.reshape(-1, width)
    expert_gate_value = matrix_product(token_rows, expert_gate_matrix)
    expert_up_value = matrix_product(token_rows, expert_up_matrix)
    expert_act = (jax.nn.silu(expert_gate_value) * expert_up_value).astype(jnp.bfloat16)
    expert_output = matrix_product(expert_act, edown_w).astype(jnp.bfloat16)
    returned = lax.all_to_all(
        expert_output.reshape(received.shape), "fsdp", split_axis=0, concat_axis=0, tiled=True
    ).reshape(slot_total, width)
    zero_row = jnp.zeros((1, width), jnp.bfloat16)
    pair_out = (
        jnp.concatenate([returned, zero_row], axis=0)[dest]
        .astype(jnp.float32)
        .reshape(tok_count, TOPK, width)
    )
    kept_pairs = kept.reshape(tok_count, TOPK).astype(jnp.float32)
    pair_weight = chosen * kept_pairs
    routed = jnp.einsum("tk,tkd->td", pair_weight, pair_out, precision=lax.Precision.HIGHEST)
    output = (middle + shared_out + routed).astype(jnp.bfloat16)
    grad_y = out_grad[0].astype(jnp.float32) * valid[:, None]
    d_chosen = jnp.sum(pair_out * grad_y[:, None, :], axis=-1) * kept_pairs
    d_gates = jnp.einsum("tk,tke->te", d_chosen, onehot, precision=lax.Precision.HIGHEST)
    d_logits = gates * (d_gates - jnp.sum(gates * d_gates, axis=-1, keepdims=True))
    pair_grad_rows = (
        (pair_weight[:, :, None] * grad_y[:, None, :])
        .reshape(pair_count, width)
        .astype(jnp.bfloat16)
    )
    send_grads = (
        jnp.zeros((slot_total + 1, width), jnp.bfloat16).at[dest].set(pair_grad_rows)[:slot_total]
    )
    grad_rows = lax.all_to_all(
        send_grads.reshape(n_experts, capacity, width),
        "fsdp",
        split_axis=0,
        concat_axis=0,
        tiled=True,
    ).reshape(-1, width)
    d_edown = matrix_product(expert_act.T, grad_rows)
    expert_activation_grad = matrix_product(grad_rows, edown_w.T)
    expert_gate_value_grad, expert_up_value_grad = swish_gradients(
        expert_activation_grad, expert_gate_value, expert_up_value
    )
    d_egate = matrix_product(token_rows.T, expert_gate_value_grad)
    expert_up_weight_grad = matrix_product(token_rows.T, expert_up_value_grad)
    row_gradients = (
        matrix_product(expert_gate_value_grad, expert_gate_matrix.T)
        + matrix_product(expert_up_value_grad, expert_up_matrix.T)
    ).astype(jnp.bfloat16)
    back_rows = lax.all_to_all(
        row_gradients.reshape(received.shape), "fsdp", split_axis=0, concat_axis=0, tiled=True
    ).reshape(slot_total, width)
    d_pairs = (
        jnp.concatenate([back_rows, zero_row], axis=0)[dest]
        .astype(jnp.float32)
        .reshape(tok_count, TOPK, width)
    )
    d_h_ffn = jnp.sum(d_pairs, axis=1)
    expert_gate_weight_gradient, expert_up_weight_gradient, expert_down_weight_gradient = (
        lax.psum_scatter(
            d_egate[None].astype(jnp.bfloat16), "ctx", scatter_dimension=1, tiled=True
        ).astype(jnp.float32),
        lax.psum_scatter(
            expert_up_weight_grad[None].astype(jnp.bfloat16), "ctx", scatter_dimension=1, tiled=True
        ).astype(jnp.float32),
        lax.psum_scatter(
            d_edown[None].astype(jnp.bfloat16), "ctx", scatter_dimension=1, tiled=True
        ).astype(jnp.float32),
    )
    d_shared_out = grad_y.astype(jnp.bfloat16)
    d_sdown = matrix_product(shared_act.T, d_shared_out)
    d_shared_act = matrix_product(d_shared_out, sdown_full.T)
    d_sgate_val, d_sup_val = swish_gradients(d_shared_act, shared_gate_val, shared_up_val)
    d_sgate = matrix_product(h_ffn.T, d_sgate_val)
    d_sup = matrix_product(h_ffn.T, d_sup_val)
    d_h_ffn = (
        d_h_ffn + matrix_product(d_sgate_val, sgate_full.T) + matrix_product(d_sup_val, sup_full.T)
    )
    d_router = jnp.dot(h_ffn.astype(jnp.float32).T, d_logits, precision=lax.Precision.HIGHEST)
    d_h_ffn = d_h_ffn + jnp.dot(
        d_logits, router_full.astype(jnp.float32).T, precision=lax.Precision.HIGHEST
    )
    d_mid_norm, d_g_ffn = norm_back(middle, feedforward_gain, d_h_ffn)
    grad_mid = grad_y + d_mid_norm
    gffn_grad, router_grad, sgate_grad, sup_grad, sdown_grad = (
        lax.psum_scatter(d_g_ffn, ("ctx", "fsdp"), scatter_dimension=0, tiled=True),
        lax.psum_scatter(d_router, ("ctx", "fsdp"), scatter_dimension=0, tiled=True),
        lax.psum_scatter(d_sgate, ("ctx", "fsdp"), scatter_dimension=0, tiled=True),
        lax.psum_scatter(d_sup, ("ctx", "fsdp"), scatter_dimension=0, tiled=True),
        lax.psum_scatter(d_sdown, ("ctx", "fsdp"), scatter_dimension=0, tiled=True),
    )
    d_attn_out = grad_mid.astype(jnp.bfloat16)
    d_wo = matrix_product(attended.T, d_attn_out)
    d_attended = matrix_product(d_attn_out, wo_full.T).astype(jnp.bfloat16)
    d_attended_heads = jnp.transpose(d_attended.reshape(tok_count, HEADS, VDIM), (1, 0, 2))

    def head_backward(items):
        query_h, nope_h, value_h, dout_h, lse_h = items
        scores, keys = head_scores(query_h, nope_h)
        probs = jnp.exp(scores - lse_h[:, None])
        d_value = matrix_product(probs.astype(jnp.bfloat16).T, dout_h)
        d_probs = matrix_product(dout_h, value_h.T)
        delta = jnp.sum(probs * d_probs, axis=-1, keepdims=True)
        d_scores = (probs * (d_probs - delta)).astype(jnp.bfloat16)
        d_query = matrix_product(d_scores, keys) * softmax_scale
        d_keys = matrix_product(d_scores.T, query_h) * softmax_scale
        return (d_query, d_keys[:, :NOPE], d_keys[:, NOPE:], d_value)

    d_query_heads, d_nope_heads, d_rope_heads, d_value_heads = lax.map(
        head_backward, (query_heads, nope_heads, value_heads, d_attended_heads, lse_heads)
    )
    d_expand_part = (
        jnp.transpose(jnp.concatenate([d_nope_heads, d_value_heads], axis=-1), (1, 0, 2))
        .reshape(seq_total, HEADS * (NOPE + VDIM))
        .astype(jnp.bfloat16)
    )
    d_rope_all = jnp.sum(d_rope_heads, axis=0)
    d_wkvb = matrix_product(latent_all.T, d_expand_part)
    d_latent_part = matrix_product(d_expand_part, wkvb_full.T)
    d_latent, d_rope = (
        lax.psum_scatter(
            d_latent_part.astype(jnp.bfloat16), "ctx", scatter_dimension=0, tiled=True
        ).astype(jnp.float32),
        lax.psum_scatter(
            d_rope_all.astype(jnp.bfloat16), "ctx", scatter_dimension=0, tiled=True
        ).astype(jnp.float32),
    )
    d_latent_raw, d_g_latent = norm_back(latent_raw, latent_gain, d_latent)
    d_rope_raw = rotate_back(d_rope, cosine, sine)
    d_latent_in = jnp.concatenate([d_latent_raw, d_rope_raw], axis=-1).astype(jnp.bfloat16)
    d_wkva = matrix_product(h_attn.T, d_latent_in)
    d_h_attn = matrix_product(d_latent_in, wkva_full.T)
    d_query = jnp.transpose(d_query_heads, (1, 0, 2))
    d_query_raw = jnp.concatenate(
        [
            d_query[..., :NOPE],
            rotate_back(d_query[..., NOPE:], cosine[:, None, :], sine[:, None, :]),
        ],
        axis=-1,
    )
    d_query_low = d_query_raw.reshape(tok_count, HEADS * (NOPE + ROPE)).astype(jnp.bfloat16)
    d_wq = matrix_product(h_attn.T, d_query_low)
    d_h_attn = d_h_attn + matrix_product(d_query_low, wq_full.T)
    d_in_norm, d_g_attn = norm_back(input_rows, attention_gain, d_h_attn)
    input_grad = (grad_mid + d_in_norm).astype(jnp.bfloat16)
    gattn_grad, wq_grad, wkva_grad, glatent_grad, wkvb_grad, wo_grad = (
        lax.psum_scatter(d_g_attn, ("ctx", "fsdp"), scatter_dimension=0, tiled=True),
        lax.psum_scatter(d_wq, ("ctx", "fsdp"), scatter_dimension=0, tiled=True),
        lax.psum_scatter(d_wkva, ("ctx", "fsdp"), scatter_dimension=0, tiled=True),
        lax.psum_scatter(d_g_latent, ("ctx", "fsdp"), scatter_dimension=0, tiled=True),
        lax.psum_scatter(d_wkvb, ("ctx", "fsdp"), scatter_dimension=0, tiled=True),
        lax.psum_scatter(d_wo, ("ctx", "fsdp"), scatter_dimension=0, tiled=True),
    )
    return (
        output[None],
        input_grad[None],
        gattn_grad,
        wq_grad,
        wkva_grad,
        glatent_grad,
        wkvb_grad,
        wo_grad,
        gffn_grad,
        router_grad,
        sgate_grad,
        sup_grad,
        sdown_grad,
        expert_gate_weight_gradient,
        expert_up_weight_gradient,
        expert_down_weight_gradient,
    )


ALL = ("y", "z", "x", "c")
PLANE = ("y", "x", "c")
FSDP = ("z", "x", "c")
BF = jnp.bfloat16
F32 = jnp.float32
PAIRS = 8
SEQ_BLOCKS = 2


def swap(value, axis):
    return lax.ppermute(value, axis, [(0, 1), (1, 0)])


def swap_zq(value):
    pairs = [(z * 4 + q, q * 4 + z) for z in range(4) for q in range(4)]
    return lax.ppermute(value, FSDP, pairs)


def spread(value, axes):
    return lax.all_to_all(value, axes, split_axis=0, concat_axis=0, tiled=True)


def gather_z(value):
    return spread(jnp.broadcast_to(value[None], (4,) + value.shape), "z")


def plane_gather(block):
    half = block.shape[0] // 2
    by_x = swap(block, "x")
    by_y = swap(block, "y")
    diag_x = swap(by_y[:half], "x")
    diag_y = swap(by_x[half:], "y")
    near = jnp.concatenate([block, by_x, by_y, diag_x, diag_y], axis=0)
    far = swap(near, "c")
    return jnp.concatenate([near, far], axis=0)


def plane_reduce(part):
    rows = part.shape[0] // 8
    half = rows // 2
    got = swap(part[4 * rows :], "c")
    total = part[: 4 * rows].astype(F32) + got.astype(F32)
    own = total[:rows]
    to_x = total[rows : 2 * rows]
    to_y = total[2 * rows : 3 * rows]
    diag = total[3 * rows :].astype(BF)
    got_x = swap(diag[:half], "x").astype(F32)
    got_y = swap(diag[half:], "y").astype(F32)
    to_y = jnp.concatenate([to_y[:half] + got_x, to_y[half:]], axis=0).astype(BF)
    to_x = jnp.concatenate([to_x[:half], to_x[half:] + got_y], axis=0).astype(BF)
    return own + swap(to_x, "x").astype(F32) + swap(to_y, "y").astype(F32)


def dot_nt(left, right):
    return lax.dot_general(left, right, (((1,), (1,)), ((), ())), preferred_element_type=F32)


def dot_tn(left, right):
    return lax.dot_general(left, right, (((0,), (0,)), ((), ())), preferred_element_type=F32)


def attention_probs(meta, seq, query, expand, rope_ref, head):
    count = query.shape[0]
    half = count // 2
    keys = jnp.concatenate(
        [expand[:, 256 * head : 256 * head + 128], rope_ref[0, :, head].reshape(count, 128)], axis=1
    )
    rows = lax.broadcasted_iota(jnp.int32, (count, count), 0)
    cols = lax.broadcasted_iota(jnp.int32, (count, count), 1)
    own = meta[4]
    row_pos = jnp.where(rows < half, rows + own * half, rows - half + (1 - own) * half)
    col_pos = jnp.where(cols < half, cols + own * half, cols - half + (1 - own) * half)
    allowed = (col_pos <= row_pos) & (col_pos < meta[seq])
    queries = jnp.concatenate(
        [query[:, 128 * head : 128 * head + 128], query[:, 256:384]], axis=1
    )
    scores = dot_nt(queries, keys) * (NOPE + ROPE) ** (-0.5)
    scores = jnp.where(allowed, scores, NEGATIVE_FILL)
    expo = jnp.exp(scores - jnp.max(scores, axis=-1, keepdims=True))
    probs = expo / jnp.sum(expo, axis=-1, keepdims=True)
    return probs, queries, keys


def attend_kernel(meta, query_ref, expand_ref, rope_ref, out_ref):
    seq = pl.program_id(0) * 2 + pl.program_id(1)
    half = query_ref.shape[2]
    query = query_ref[0].reshape(2 * half, 384)
    expand = expand_ref[0].reshape(2 * half, 512)
    for head in range(2):
        probs, _, _ = attention_probs(meta, seq, query, expand, rope_ref, head)
        values = expand[:, 256 * head + 128 : 256 * head + 256]
        attended = jnp.dot(probs.astype(BF), values, preferred_element_type=F32).astype(BF)
        out_ref[0, :, :, 128 * head : 128 * head + 128] = attended.reshape(2, half, 128)


def attend_back_kernel(
    meta, query_ref, expand_ref, rope_ref, dout_ref, cos_ref, sin_ref, dq_ref, dkv_ref, dkr_ref
):
    seq = pl.program_id(0) * 2 + pl.program_id(1)
    half = query_ref.shape[2]
    count = 2 * half
    scale = (NOPE + ROPE) ** (-0.5)
    query = query_ref[0].reshape(count, 384)
    expand = expand_ref[0].reshape(count, 512)
    dout = dout_ref[0].reshape(count, 256)
    cosine = cos_ref[0].reshape(count, 128)
    sine = sin_ref[0].reshape(count, 128)
    lane = lax.broadcasted_iota(jnp.int32, (count, 128), 1)
    first = (lane % 64) < 32
    dq_rope = jnp.zeros((count, 128), F32)
    dk_rope = jnp.zeros((count, 128), F32)
    for head in range(2):
        probs, queries, keys = attention_probs(meta, seq, query, expand, rope_ref, head)
        values = expand[:, 256 * head + 128 : 256 * head + 256]
        dout_h = dout[:, 128 * head : 128 * head + 128]
        d_value = dot_tn(probs.astype(BF), dout_h)
        d_probs = dot_nt(dout_h, values)
        delta = jnp.sum(probs * d_probs, axis=-1, keepdims=True)
        d_scores = (probs * (d_probs - delta)).astype(BF)
        d_query = jnp.dot(d_scores, keys, preferred_element_type=F32) * scale
        d_keys = dot_tn(d_scores, queries) * scale
        dq_ref[0, :, :, 128 * head : 128 * head + 128] = (
            d_query[:, :128].astype(BF).reshape(2, half, 128)
        )
        dq_rope = dq_rope + d_query[:, 128:]
        dk_rope = dk_rope + jnp.where(first == (head == 0), d_keys[:, 128:], 0.0)
        dkv_ref[0, :, :, 256 * head : 256 * head + 128] = (
            d_keys[:, :128].astype(BF).reshape(2, half, 128)
        )
        dkv_ref[0, :, :, 256 * head + 128 : 256 * head + 256] = d_value.astype(BF).reshape(
            2, half, 128
        )
    dq_rope = dq_rope * cosine - pltpu.roll(dq_rope, 64, 1) * sine
    dq_ref[0, :, :, 256:384] = dq_rope.astype(BF).reshape(2, half, 128)
    dkr_ref[0] = dk_rope.reshape(2, half, 128)


def seq_spec(half, width):
    return pl.BlockSpec((1, 2, half, width), lambda c, x, meta: (c, 0, x, 0))


def attend(meta, query, expand, ropes):
    half = query.shape[0] // 8
    grid_spec = pltpu.PrefetchScalarGridSpec(
        num_scalar_prefetch=1,
        grid=(2, 2),
        in_specs=[
            seq_spec(half, 384),
            seq_spec(half, 512),
            pl.BlockSpec((1, 2, 2, half, 128), lambda c, x, meta: (c, 0, 0, x, 0)),
        ],
        out_specs=seq_spec(half, 256),
    )
    return pl.pallas_call(
        attend_kernel,
        grid_spec=grid_spec,
        out_shape=jax.ShapeDtypeStruct((2, 2, 2 * half, 256), BF),
        name="attend",
    )(
        meta,
        query.reshape(2, 2, 2 * half, 384),
        expand.reshape(2, 2, 2 * half, 512),
        ropes,
    ).reshape(8 * half, 256)


def attend_back(meta, query, expand, ropes, dout, cosine, sine):
    half = query.shape[0] // 8
    grid_spec = pltpu.PrefetchScalarGridSpec(
        num_scalar_prefetch=1,
        grid=(2, 2),
        in_specs=[
            seq_spec(half, 384),
            seq_spec(half, 512),
            pl.BlockSpec((1, 2, 2, half, 128), lambda c, x, meta: (c, 0, 0, x, 0)),
            seq_spec(half, 256),
            seq_spec(half, 128),
            seq_spec(half, 128),
        ],
        out_specs=[seq_spec(half, 384), seq_spec(half, 512), seq_spec(half, 128)],
    )
    d_query, d_expand, d_rope = pl.pallas_call(
        attend_back_kernel,
        grid_spec=grid_spec,
        out_shape=[
            jax.ShapeDtypeStruct((2, 2, 2 * half, 384), BF),
            jax.ShapeDtypeStruct((2, 2, 2 * half, 512), BF),
            jax.ShapeDtypeStruct((2, 2, 2 * half, 128), F32),
        ],
        name="attend_back",
    )(
        meta,
        query.reshape(2, 2, 2 * half, 384),
        expand.reshape(2, 2, 2 * half, 512),
        ropes,
        dout.reshape(2, 2, 2 * half, 256),
        cosine.reshape(2, 2, 2 * half, 128),
        sine.reshape(2, 2, 2 * half, 128),
    )
    return (
        d_query.reshape(8 * half, 384),
        d_expand.reshape(8 * half, 512),
        d_rope.reshape(8 * half, 128),
    )


def pick_kernel(pick_ref, rows_ref, out_ref):
    out_ref[0] = jnp.dot(pick_ref[0], rows_ref[0], preferred_element_type=F32).astype(BF)


def pick_rows(pick, rows):
    blocks, cap, count = pick.shape
    width = rows.shape[-1]
    return pl.pallas_call(
        pick_kernel,
        grid=(blocks,),
        in_specs=[
            pl.BlockSpec((1, cap, count), lambda b: (b, 0, 0)),
            pl.BlockSpec((1, count, width), lambda b: (b, 0, 0)),
        ],
        out_specs=pl.BlockSpec((1, cap, width), lambda b: (b, 0, 0)),
        out_shape=jax.ShapeDtypeStruct((blocks, cap, width), BF),
        name="pick_rows",
    )(pick, rows.reshape(blocks, count, width)).reshape(blocks * cap, width)


def merge_kernel(left_ref, right_ref, pick_ref, rows_ref, out_ref):
    total = jnp.dot(left_ref[...], right_ref[...], preferred_element_type=F32)
    out_ref[...] = (total + dot_tn(pick_ref[0], rows_ref[0])).astype(BF)


def merge_rows(left, right, pick, rows):
    blocks, cap, count = pick.shape
    depth, width = right.shape
    return pl.pallas_call(
        merge_kernel,
        grid=(blocks,),
        in_specs=[
            pl.BlockSpec((count, depth), lambda b: (b, 0)),
            pl.BlockSpec((depth, width), lambda b: (0, 0)),
            pl.BlockSpec((1, cap, count), lambda b: (b, 0, 0)),
            pl.BlockSpec((1, cap, width), lambda b: (b, 0, 0)),
        ],
        out_specs=pl.BlockSpec((count, width), lambda b: (b, 0)),
        out_shape=jax.ShapeDtypeStruct((blocks * count, width), BF),
        name="merge_rows",
    )(left, right, pick, rows.reshape(blocks, cap, width))


def local_tokens(
    tokens,
    attn_norm,
    w_query,
    w_latent,
    latent_norm,
    w_expand,
    w_output,
    ffn_norm,
    w_router,
    shared_gate,
    shared_up,
    shared_down,
    expert_gate,
    expert_up,
    expert_down,
    out_grad,
    seq_length,
    expert_ids,
    fill_order,
):
    tok = tokens.shape[1]
    width = tokens.shape[2]
    n_dev = 32
    n_experts = 16
    n_blocks = n_dev
    capacity = tok * TOPK // n_experts
    pair_count = tok * TOPK
    my_y = lax.axis_index("y")
    my_x = lax.axis_index("x")
    my_c = lax.axis_index("c")
    my_z = lax.axis_index("z")
    own_tokens = tokens[0]
    input_rows = own_tokens.astype(F32)

    route_ids = expert_ids[0]
    flat_ids = route_ids.reshape(pair_count)
    ranks = slot_rank(flat_ids, fill_order[0]).reshape(tok, TOPK)
    kept = ranks < capacity
    same = route_ids[:, :, None] == jnp.arange(n_experts, dtype=jnp.int32)[None, None, :]
    slot_plus = jnp.sum(
        jnp.where(same & kept[:, :, None], ranks[:, :, None] + 1, 0), axis=1
    )
    slot_table = (slot_plus - 1).astype(BF)

    n_small = [tok, attn_norm.shape[0], ffn_norm.shape[0], latent_norm.shape[0], 16, w_router.size]
    small_all = jnp.concatenate(
        [
            attn_norm,
            ffn_norm,
            latent_norm,
            jnp.broadcast_to(seq_length.astype(BF), (16,)),
            w_router.reshape(-1),
        ]
    )
    to_each = jnp.concatenate(
        [
            jnp.concatenate([slot_table.T, slot_table.T], axis=0),
            jnp.broadcast_to(small_all[None], (n_dev, small_all.shape[0])),
        ],
        axis=1,
    )
    small = spread(to_each, ALL)
    cuts = [sum(n_small[: i + 1]) for i in range(len(n_small))]
    slot_of = small[:, : cuts[0]]
    attention_gain = small[:, cuts[0] : cuts[1]].reshape(-1).astype(F32)
    feedforward_gain = small[:, cuts[1] : cuts[2]].reshape(-1).astype(F32)
    latent_gain = small[:, cuts[2] : cuts[3]].reshape(-1).astype(F32)
    lengths = small[:16, cuts[3]].astype(jnp.int32)
    router = small[:, cuts[4] : cuts[5]].reshape(width, n_experts)

    def head_columns(value):
        rows = value.shape[0]
        view = value.reshape(rows, PAIRS, 2, NOPE + ROPE)
        nope = view[..., :NOPE].reshape(rows, PAIRS, 2 * NOPE)
        rope = view[..., NOPE:].reshape(rows, PAIRS, 2, 2, ROPE // 2)
        rope = jnp.transpose(rope, (0, 1, 3, 2, 4)).reshape(rows, PAIRS, 2 * ROPE)
        return jnp.concatenate([nope, rope], axis=-1)

    def by_pair(value):
        return jnp.transpose(value, (1, 0, 2))

    def natural_rows(value):
        rows = value.shape[2]
        view = value.reshape(4, 2, 4, rows, value.shape[-1])
        return jnp.transpose(view, (1, 0, 2, 3, 4)).reshape(n_dev * rows, value.shape[-1])

    wq = natural_rows(gather_z(spread(by_pair(head_columns(w_query)), PLANE)))
    we = natural_rows(
        gather_z(spread(by_pair(w_expand.reshape(w_expand.shape[0], PAIRS, 512)), PLANE))
    )
    wo = gather_z(swap_zq(w_output)).reshape(2 * VDIM, width)
    wl = lax.all_gather(w_latent, ALL, axis=0, tiled=True)

    plane_tokens = plane_gather(own_tokens)
    h_attn = rms_norm(plane_tokens.astype(F32), attention_gain).astype(BF)
    half_pos = jnp.arange(tok, dtype=jnp.int32)
    pos_own = my_y * tok + half_pos
    pos_far = (1 - my_y) * tok + half_pos
    cos_own, sin_own = rope_tables(pos_own, ROPE)
    cos_far, sin_far = rope_tables(pos_far, ROPE)

    def plane_rows(own, far):
        return jnp.concatenate([own, own, far, far] * 2, axis=0)

    cos_rows = plane_rows(cos_own, cos_far)
    sin_rows = plane_rows(sin_own, sin_far)
    cos_pair = jnp.concatenate([cos_rows] * 4, axis=1)
    sin_pair = jnp.concatenate([-sin_rows, -sin_rows, sin_rows, sin_rows], axis=1)
    query_raw = matrix_product(h_attn, wq)
    query_rope = query_raw[:, 256:]
    query_rope_swapped = jnp.concatenate([query_rope[:, 64:], query_rope[:, :64]], axis=1)
    query = jnp.concatenate(
        [query_raw[:, :256], query_rope * cos_pair + query_rope_swapped * sin_pair], axis=1
    ).astype(BF)
    latent_in = matrix_product(h_attn, wl)
    latent = rms_norm(latent_in[:, :KVR], latent_gain).astype(BF)
    key_rope = rotate(latent_in[:, KVR:], cos_rows, sin_rows).astype(BF)
    key_a, key_b = key_rope[:, :32], key_rope[:, 32:]
    blank = jnp.zeros_like(key_a)
    ropes = jnp.stack(
        [
            jnp.concatenate([key_a, blank, key_b, blank], axis=1).reshape(2, 2, 2 * tok, 128),
            jnp.concatenate([blank, key_a, blank, key_b], axis=1).reshape(2, 2, 2 * tok, 128),
        ],
        axis=2,
    )
    expand = matrix_product(latent, we).astype(BF)
    my_seq = my_z * 4 + my_x * 2 + my_c
    meta = jnp.stack(
        [
            lengths[my_seq],
            lengths[my_z * 4 + (1 - my_x) * 2 + my_c],
            lengths[my_z * 4 + my_x * 2 + (1 - my_c)],
            lengths[my_z * 4 + (1 - my_x) * 2 + (1 - my_c)],
            my_y.astype(jnp.int32),
        ]
    )
    attended = attend(meta, query, expand, ropes)
    middle = input_rows + plane_reduce(matrix_product(attended, wo).astype(BF))

    h_ffn = rms_norm(middle, feedforward_gain).astype(BF)
    gates = jax.nn.softmax(matrix_product(h_ffn, router), axis=-1)
    valid = (pos_own < seq_length[0]).astype(F32)
    grad_y = out_grad[0].astype(F32) * valid[:, None]
    grad_low = grad_y.astype(BF)
    all_grad = lax.all_gather(grad_low, ALL, axis=0, tiled=True)
    all_ffn = lax.all_gather(h_ffn, ALL, axis=0, tiled=True)
    gate_of = spread(jnp.concatenate([gates.T, gates.T], axis=0), ALL)

    n_shared = shared_down.shape[0]

    def hidden_columns(value):
        return jnp.transpose(value.reshape(value.shape[0], n_dev, n_shared), (1, 0, 2))

    shared_in = spread(
        jnp.concatenate([hidden_columns(shared_gate), hidden_columns(shared_up)], axis=2), ALL
    ).reshape(width, 2 * n_shared)

    def half_columns(value):
        return lax.all_to_all(value[0], "y", split_axis=1, concat_axis=0, tiled=True)

    gate_w = half_columns(expert_gate)
    up_w = half_columns(expert_up)
    down_w = expert_down[0]

    slots = lax.broadcasted_iota(jnp.int32, (n_blocks, capacity, tok), 1)
    taken = slot_of.astype(jnp.int32)[:, None, :] == slots
    pick = taken.astype(BF)
    rows = pick_rows(pick, all_ffn)
    grad_rows = pick_rows(pick, all_grad)
    gate_slot = jnp.sum(jnp.where(taken, gate_of[:, None, :], 0.0), axis=2).reshape(-1, 1)
    gate_val = matrix_product(rows, gate_w)
    up_val = matrix_product(rows, up_w)
    act = jax.nn.silu(gate_val) * up_val
    act_weighted = (act * gate_slot).astype(BF)
    d_act = dot_nt(grad_rows, down_w)
    d_gate_slot = jnp.sum(act * d_act, axis=1)
    d_gate_val, d_up_val = swish_gradients(d_act * gate_slot, gate_val, up_val)
    pair_rows = matrix_product(act_weighted, down_w).astype(BF)
    d_rows = (dot_nt(d_gate_val, gate_w) + dot_nt(d_up_val, up_w)).astype(BF)

    shared_val = matrix_product(all_ffn, shared_in)
    shared_gate_val = shared_val[:, :n_shared]
    shared_up_val = shared_val[:, n_shared:]
    shared_act = (jax.nn.silu(shared_gate_val) * shared_up_val).astype(BF)
    d_shared_act = dot_nt(all_grad, shared_down)
    d_sgate_val, d_sup_val = swish_gradients(d_shared_act, shared_gate_val, shared_up_val)
    d_shared_val = jnp.concatenate([d_sgate_val, d_sup_val], axis=1)

    d_gate_of = jnp.sum(
        jnp.where(taken, d_gate_slot.reshape(n_blocks, capacity)[:, :, None], 0.0), axis=1
    )
    d_chosen = spread(d_gate_of, ALL)
    d_gates = (d_chosen[:n_experts] + d_chosen[n_experts:]).T

    dh_part = merge_rows(d_shared_val, shared_in.T, pick, d_rows)
    d_h_ffn = lax.psum_scatter(dh_part, ALL, scatter_dimension=0, tiled=True).astype(F32)
    out_part = merge_rows(shared_act, shared_down, pick, pair_rows)
    output = (
        middle + lax.psum_scatter(out_part, ALL, scatter_dimension=0, tiled=True).astype(F32)
    ).astype(BF)

    d_down_w = dot_tn(act_weighted, grad_rows)
    d_gate_w = dot_tn(rows, d_gate_val).astype(BF)
    d_up_w = dot_tn(rows, d_up_val).astype(BF)

    def whole_columns(value):
        return lax.all_to_all(value, "y", split_axis=0, concat_axis=1, tiled=True).astype(F32)

    d_expert_gate = whole_columns(d_gate_w)
    d_expert_up = whole_columns(d_up_w)
    d_shared_down = dot_tn(shared_act, all_grad)
    d_shared_in = spread(
        dot_tn(all_ffn, d_shared_val).astype(BF).reshape(n_dev, width // n_dev, 2 * n_shared), ALL
    ).astype(F32)

    def shared_columns(value):
        return jnp.transpose(value, (1, 0, 2)).reshape(width // n_dev, n_dev * n_shared)

    d_shared_gate = shared_columns(d_shared_in[..., :n_shared])
    d_shared_up = shared_columns(d_shared_in[..., n_shared:])

    d_logits = gates * (d_gates - jnp.sum(gates * d_gates, axis=-1, keepdims=True))
    d_router = jnp.dot(h_ffn.astype(F32).T, d_logits, precision=lax.Precision.HIGHEST)
    d_h_ffn = d_h_ffn + jnp.dot(
        d_logits, router.astype(F32).T, precision=lax.Precision.HIGHEST
    )
    d_mid_norm, d_g_ffn = norm_back(middle, feedforward_gain, d_h_ffn)
    grad_mid = grad_y + d_mid_norm
    early = jnp.sum(
        spread(
            jnp.concatenate([d_g_ffn.reshape(n_dev, -1), d_router.reshape(n_dev, -1)], axis=1), ALL
        ),
        axis=0,
    )
    gffn_grad = early[: width // n_dev]
    router_grad = early[width // n_dev :].reshape(width // n_dev, n_experts)

    plane_dout = plane_gather(grad_mid.astype(BF))

    def reduce_z(value):
        got = spread(value.astype(BF), "z")
        return jnp.sum(got.astype(F32), axis=0).astype(BF)

    def to_owners(value, rows_each):
        view = value.reshape(2, 4, 4, rows_each, value.shape[-1])
        view = jnp.transpose(view, (1, 0, 2, 3, 4)).reshape(4, 8, rows_each, value.shape[-1])
        return jnp.transpose(spread(reduce_z(view), PLANE).astype(F32), (1, 0, 2))

    d_wo = dot_tn(attended, plane_dout)
    wo_grad = swap_zq(reduce_z(d_wo.reshape(4, -1, width))).astype(F32)
    d_attended = dot_nt(plane_dout, wo).astype(BF)
    d_query, d_expand, d_rope = attend_back(
        meta, query, expand, ropes, d_attended, cos_pair, sin_pair
    )
    d_latent_part = dot_nt(d_expand, we)
    d_rope = jnp.concatenate(
        [d_rope[:, :32] + d_rope[:, 32:64], d_rope[:, 64:96] + d_rope[:, 96:]], axis=1
    )
    d_low = plane_reduce(jnp.concatenate([d_latent_part, d_rope], axis=1).astype(BF))
    d_latent_raw, d_g_latent = norm_back(latent_in[:tok, :KVR], latent_gain, d_low[:, :KVR])
    d_rope_raw = rotate_back(d_low[:, KVR:], cos_own, sin_own)
    d_latent_in = jnp.concatenate([d_latent_raw, d_rope_raw], axis=-1).astype(BF)
    d_hattn = plane_reduce(dot_nt(d_query, wq).astype(BF)) + dot_nt(d_latent_in, wl)
    d_wl = dot_tn(h_attn[:tok], d_latent_in).astype(BF)
    wl_grad = lax.psum_scatter(d_wl, ALL, scatter_dimension=0, tiled=True).astype(F32)
    we_grad = to_owners(dot_tn(latent, d_expand), w_expand.shape[0]).reshape(w_expand.shape)
    wq_grad = to_owners(dot_tn(h_attn, d_query), w_query.shape[0])
    d_nope = wq_grad[..., : 2 * NOPE].reshape(-1, PAIRS, 2, NOPE)
    d_wrope = wq_grad[..., 2 * NOPE :].reshape(-1, PAIRS, 2, 2, ROPE // 2)
    d_wrope = jnp.transpose(d_wrope, (0, 1, 3, 2, 4)).reshape(-1, PAIRS, 2, ROPE)
    wq_grad = jnp.concatenate([d_nope, d_wrope], axis=-1).reshape(w_query.shape)
    d_in_norm, d_g_attn = norm_back(input_rows, attention_gain, d_hattn)
    input_grad = (grad_mid + d_in_norm).astype(BF)
    late = jnp.sum(
        spread(
            jnp.concatenate([d_g_attn.reshape(n_dev, -1), d_g_latent.reshape(n_dev, -1)], axis=1),
            ALL,
        ),
        axis=0,
    )
    return (
        output[None],
        input_grad[None],
        late[: width // n_dev],
        wq_grad,
        wl_grad,
        late[width // n_dev :],
        we_grad,
        wo_grad,
        gffn_grad,
        router_grad,
        d_shared_gate,
        d_shared_up,
        d_shared_down,
        d_expert_gate[None],
        d_expert_up[None],
        d_down_w[None],
    )


def tokens_plan(mesh):
    fine = Mesh(mesh.devices.reshape(2, 4, 2, 2), ALL)
    rows = P(FSDP, "y", None)
    vector = P(ALL)
    matrix = P(ALL, None)
    in_specs = (
        rows,
        vector,
        matrix,
        matrix,
        vector,
        matrix,
        matrix,
        vector,
        matrix,
        matrix,
        matrix,
        matrix,
        rows,
        rows,
        rows,
        rows,
        P(FSDP),
        rows,
        P(FSDP, "y"),
    )
    out_specs = (
        rows,
        rows,
        vector,
        matrix,
        matrix,
        vector,
        matrix,
        matrix,
        vector,
        matrix,
        matrix,
        matrix,
        matrix,
        rows,
        rows,
        rows,
    )
    return jax.shard_map(
        local_tokens, mesh=fine, in_specs=in_specs, out_specs=out_specs, check_vma=False
    )


def weights_plan(mesh):
    in_specs = (
        P("fsdp", "ctx", None),
        P(("ctx", "fsdp")),
        P(("ctx", "fsdp"), None),
        P(("ctx", "fsdp"), None),
        P(("ctx", "fsdp")),
        P(("ctx", "fsdp"), None),
        P(("ctx", "fsdp"), None),
        P(("ctx", "fsdp")),
        P(("ctx", "fsdp"), None),
        P(("ctx", "fsdp"), None),
        P(("ctx", "fsdp"), None),
        P(("ctx", "fsdp"), None),
        P("fsdp", "ctx", None),
        P("fsdp", "ctx", None),
        P("fsdp", "ctx", None),
        P("fsdp", "ctx", None),
        P("fsdp"),
        P("fsdp", "ctx", None),
        P("fsdp", "ctx"),
    )
    out_specs = (
        P("fsdp", "ctx", None),
        P("fsdp", "ctx", None),
        P(("ctx", "fsdp")),
        P(("ctx", "fsdp"), None),
        P(("ctx", "fsdp"), None),
        P(("ctx", "fsdp")),
        P(("ctx", "fsdp"), None),
        P(("ctx", "fsdp"), None),
        P(("ctx", "fsdp")),
        P(("ctx", "fsdp"), None),
        P(("ctx", "fsdp"), None),
        P(("ctx", "fsdp"), None),
        P(("ctx", "fsdp"), None),
        P("fsdp", "ctx", None),
        P("fsdp", "ctx", None),
        P("fsdp", "ctx", None),
    )
    return jax.shard_map(local_weights, mesh=mesh, in_specs=in_specs, out_specs=out_specs, check_vma=False)


def solution(mesh):
    if mesh.shape["ctx"] == 2 and mesh.shape["fsdp"] == 16:
        return tokens_plan(mesh)
    return weights_plan(mesh)
```

```python
import jax
import jax.numpy as jnp
from jax import lax
from jax.experimental import pallas as pl
from jax.experimental.pallas import tpu as pltpu
from jax.sharding import Mesh
from jax.sharding import PartitionSpec as P

HEADS = 16
NOPE = 128
ROPE = 64
VDIM = 128
KVR = 512
TOPK = 6


EPSILON = 1e-06
ROPE_BASE = 10000.0
NEGATIVE_FILL = -1e30


def matrix_product(left, right):
    return jnp.dot(left, right, preferred_element_type=jnp.float32)


def rms_norm(values, gain):
    return values * lax.rsqrt(jnp.mean(values * values, axis=-1, keepdims=True) + EPSILON) * gain


def norm_back(values, gain, grad_out):
    inverse = lax.rsqrt(jnp.mean(values * values, axis=-1, keepdims=True) + EPSILON)
    normed = values * inverse
    gain_grad = jnp.sum(grad_out * normed, axis=0)
    scaled = grad_out * gain
    input_grad = inverse * (scaled - normed * jnp.mean(scaled * normed, axis=-1, keepdims=True))
    return (input_grad, gain_grad)


def rope_tables(positions, width):
    half = width // 2
    freqs = ROPE_BASE ** (-jnp.arange(half, dtype=jnp.float32) / half)
    angles = positions.astype(jnp.float32)[:, None] * freqs[None, :]
    return (jnp.cos(angles), jnp.sin(angles))


def rotate(values, cosine, sine):
    half = values.shape[-1] // 2
    first = values[..., :half]
    second = values[..., half:]
    return jnp.concatenate(
        [first * cosine - second * sine, second * cosine + first * sine], axis=-1
    )


def rotate_back(grads, cosine, sine):
    half = grads.shape[-1] // 2
    first = grads[..., :half]
    second = grads[..., half:]
    return jnp.concatenate(
        [first * cosine + second * sine, second * cosine - first * sine], axis=-1
    )


def slot_rank(expert_flat, priority):
    same = (expert_flat[:, None] == expert_flat[None, :]) & (priority[None, :] < priority[:, None])
    return jnp.sum(same.astype(jnp.int32), axis=1)


def swish_gradients(d_act, gate_val, up_val):
    sigma = jax.nn.sigmoid(gate_val)
    d_gate = (d_act * up_val * sigma * (1.0 + gate_val * (1.0 - sigma))).astype(jnp.bfloat16)
    d_up = (d_act * gate_val * sigma).astype(jnp.bfloat16)
    return (d_gate, d_up)


def local_weights(
    tokens,
    attn_norm,
    w_query,
    w_latent,
    latent_norm,
    w_expand,
    w_output,
    ffn_norm,
    w_router,
    shared_gate,
    shared_up,
    shared_down,
    expert_gate,
    expert_up,
    expert_down,
    out_grad,
    seq_length,
    expert_ids,
    fill_order,
):
    input_rows = tokens[0].astype(jnp.float32)
    tok_count = input_rows.shape[0]
    width = input_rows.shape[1]
    n_experts = expert_gate.shape[0] * lax.axis_size("fsdp")
    capacity = tok_count * TOPK // n_experts
    pair_count = tok_count * TOPK
    softmax_scale = (NOPE + ROPE) ** (-0.5)
    positions = lax.axis_index("ctx") * tok_count + jnp.arange(tok_count, dtype=jnp.int32)
    seq_used = seq_length[0]
    valid = (positions < seq_used).astype(jnp.float32)
    cosine, sine = rope_tables(positions, ROPE)
    attention_gain, wq_full, wkva_full, latent_gain, wkvb_full, wo_full = (
        lax.all_gather(attn_norm, ("ctx", "fsdp"), axis=0, tiled=True),
        lax.all_gather(w_query, ("ctx", "fsdp"), axis=0, tiled=True),
        lax.all_gather(w_latent, ("ctx", "fsdp"), axis=0, tiled=True),
        lax.all_gather(latent_norm, ("ctx", "fsdp"), axis=0, tiled=True),
        lax.all_gather(w_expand, ("ctx", "fsdp"), axis=0, tiled=True),
        lax.all_gather(w_output, ("ctx", "fsdp"), axis=0, tiled=True),
    )
    attention_gain = attention_gain.astype(jnp.float32)
    latent_gain = latent_gain.astype(jnp.float32)
    h_attn = rms_norm(input_rows, attention_gain).astype(jnp.bfloat16)
    query_raw = matrix_product(h_attn, wq_full).reshape(tok_count, HEADS, NOPE + ROPE)
    query_rot = jnp.concatenate(
        [
            query_raw[..., :NOPE],
            rotate(query_raw[..., NOPE:], cosine[:, None, :], sine[:, None, :]),
        ],
        axis=-1,
    ).astype(jnp.bfloat16)
    latent_in = matrix_product(h_attn, wkva_full)
    latent_raw = latent_in[:, :KVR]
    latent = rms_norm(latent_raw, latent_gain).astype(jnp.bfloat16)
    key_rope = rotate(latent_in[:, KVR:], cosine, sine).astype(jnp.bfloat16)
    latent_all, rope_all = (
        lax.all_gather(latent, "ctx", axis=0, tiled=True),
        lax.all_gather(key_rope, "ctx", axis=0, tiled=True),
    )
    expand_all = matrix_product(latent_all, wkvb_full).astype(jnp.bfloat16)
    seq_total = expand_all.shape[0]
    expand_heads = jnp.transpose(expand_all.reshape(seq_total, HEADS, NOPE + VDIM), (1, 0, 2))
    nope_heads = expand_heads[..., :NOPE]
    value_heads = expand_heads[..., NOPE:]
    query_heads = jnp.transpose(query_rot, (1, 0, 2))
    key_pos = jnp.arange(seq_total, dtype=jnp.int32)
    allowed = (key_pos[None, :] <= positions[:, None]) & (key_pos[None, :] < seq_used)

    def head_scores(query_h, nope_h):
        keys = jnp.concatenate([nope_h, rope_all], axis=-1)
        scores = matrix_product(query_h, keys.T) * softmax_scale
        return (jnp.where(allowed, scores, NEGATIVE_FILL), keys)

    def head_forward(items):
        query_h, nope_h, value_h = items
        scores, keys = head_scores(query_h, nope_h)
        highest_score = jnp.max(scores, axis=-1, keepdims=True)
        expo = jnp.exp(scores - highest_score)
        total = jnp.sum(expo, axis=-1, keepdims=True)
        probs = (expo / total).astype(jnp.bfloat16)
        attended_h = matrix_product(probs, value_h).astype(jnp.bfloat16)
        return (attended_h, highest_score[:, 0] + jnp.log(total[:, 0]))

    attended_heads, lse_heads = lax.map(head_forward, (query_heads, nope_heads, value_heads))
    attended = jnp.transpose(attended_heads, (1, 0, 2)).reshape(tok_count, HEADS * VDIM)
    middle = input_rows + matrix_product(attended, wo_full)
    feedforward_gain, router_full, sgate_full, sup_full, sdown_full = (
        lax.all_gather(ffn_norm, ("ctx", "fsdp"), axis=0, tiled=True),
        lax.all_gather(w_router, ("ctx", "fsdp"), axis=0, tiled=True),
        lax.all_gather(shared_gate, ("ctx", "fsdp"), axis=0, tiled=True),
        lax.all_gather(shared_up, ("ctx", "fsdp"), axis=0, tiled=True),
        lax.all_gather(shared_down, ("ctx", "fsdp"), axis=0, tiled=True),
    )
    feedforward_gain = feedforward_gain.astype(jnp.float32)
    expert_gate_gathered, expert_up_gathered, expert_down_gathered = (
        lax.all_gather(expert_gate, "ctx", axis=1, tiled=True),
        lax.all_gather(expert_up, "ctx", axis=1, tiled=True),
        lax.all_gather(expert_down, "ctx", axis=1, tiled=True),
    )
    expert_gate_matrix = expert_gate_gathered[0]
    expert_up_matrix = expert_up_gathered[0]
    edown_w = expert_down_gathered[0]
    h_ffn = rms_norm(middle, feedforward_gain).astype(jnp.bfloat16)
    gates = jax.nn.softmax(matrix_product(h_ffn, router_full), axis=-1)
    route_ids = expert_ids[0]
    onehot = (
        route_ids[:, :, None] == jnp.arange(n_experts, dtype=jnp.int32)[None, None, :]
    ).astype(jnp.float32)
    chosen = jnp.einsum("tke,te->tk", onehot, gates, precision=lax.Precision.HIGHEST)
    shared_gate_val = matrix_product(h_ffn, sgate_full)
    shared_up_val = matrix_product(h_ffn, sup_full)
    shared_act = (jax.nn.silu(shared_gate_val) * shared_up_val).astype(jnp.bfloat16)
    shared_out = matrix_product(shared_act, sdown_full)
    flat_ids = route_ids.reshape(pair_count)
    ranks = slot_rank(flat_ids, fill_order[0])
    kept = ranks < capacity
    dest = jnp.where(kept, flat_ids * capacity + ranks, n_experts * capacity)
    pair_token = jnp.arange(pair_count) // TOPK
    slot_total = n_experts * capacity
    send_rows = (
        jnp.zeros((slot_total + 1, width), jnp.bfloat16)
        .at[dest]
        .set(h_ffn[pair_token])[:slot_total]
    )
    received = lax.all_to_all(
        send_rows.reshape(n_experts, capacity, width),
        "fsdp",
        split_axis=0,
        concat_axis=0,
        tiled=True,
    )
    token_rows = received.reshape(-1, width)
    expert_gate_value = matrix_product(token_rows, expert_gate_matrix)
    expert_up_value = matrix_product(token_rows, expert_up_matrix)
    expert_act = (jax.nn.silu(expert_gate_value) * expert_up_value).astype(jnp.bfloat16)
    expert_output = matrix_product(expert_act, edown_w).astype(jnp.bfloat16)
    returned = lax.all_to_all(
        expert_output.reshape(received.shape), "fsdp", split_axis=0, concat_axis=0, tiled=True
    ).reshape(slot_total, width)
    zero_row = jnp.zeros((1, width), jnp.bfloat16)
    pair_out = (
        jnp.concatenate([returned, zero_row], axis=0)[dest]
        .astype(jnp.float32)
        .reshape(tok_count, TOPK, width)
    )
    kept_pairs = kept.reshape(tok_count, TOPK).astype(jnp.float32)
    pair_weight = chosen * kept_pairs
    routed = jnp.einsum("tk,tkd->td", pair_weight, pair_out, precision=lax.Precision.HIGHEST)
    output = (middle + shared_out + routed).astype(jnp.bfloat16)
    grad_y = out_grad[0].astype(jnp.float32) * valid[:, None]
    d_chosen = jnp.sum(pair_out * grad_y[:, None, :], axis=-1) * kept_pairs
    d_gates = jnp.einsum("tk,tke->te", d_chosen, onehot, precision=lax.Precision.HIGHEST)
    d_logits = gates * (d_gates - jnp.sum(gates * d_gates, axis=-1, keepdims=True))
    pair_grad_rows = (
        (pair_weight[:, :, None] * grad_y[:, None, :])
        .reshape(pair_count, width)
        .astype(jnp.bfloat16)
    )
    send_grads = (
        jnp.zeros((slot_total + 1, width), jnp.bfloat16).at[dest].set(pair_grad_rows)[:slot_total]
    )
    grad_rows = lax.all_to_all(
        send_grads.reshape(n_experts, capacity, width),
        "fsdp",
        split_axis=0,
        concat_axis=0,
        tiled=True,
    ).reshape(-1, width)
    d_edown = matrix_product(expert_act.T, grad_rows)
    expert_activation_grad = matrix_product(grad_rows, edown_w.T)
    expert_gate_value_grad, expert_up_value_grad = swish_gradients(
        expert_activation_grad, expert_gate_value, expert_up_value
    )
    d_egate = matrix_product(token_rows.T, expert_gate_value_grad)
    expert_up_weight_grad = matrix_product(token_rows.T, expert_up_value_grad)
    row_gradients = (
        matrix_product(expert_gate_value_grad, expert_gate_matrix.T)
        + matrix_product(expert_up_value_grad, expert_up_matrix.T)
    ).astype(jnp.bfloat16)
    back_rows = lax.all_to_all(
        row_gradients.reshape(received.shape), "fsdp", split_axis=0, concat_axis=0, tiled=True
    ).reshape(slot_total, width)
    d_pairs = (
        jnp.concatenate([back_rows, zero_row], axis=0)[dest]
        .astype(jnp.float32)
        .reshape(tok_count, TOPK, width)
    )
    d_h_ffn = jnp.sum(d_pairs, axis=1)
    expert_gate_weight_gradient, expert_up_weight_gradient, expert_down_weight_gradient = (
        lax.psum_scatter(
            d_egate[None].astype(jnp.bfloat16), "ctx", scatter_dimension=1, tiled=True
        ).astype(jnp.float32),
        lax.psum_scatter(
            expert_up_weight_grad[None].astype(jnp.bfloat16), "ctx", scatter_dimension=1, tiled=True
        ).astype(jnp.float32),
        lax.psum_scatter(
            d_edown[None].astype(jnp.bfloat16), "ctx", scatter_dimension=1, tiled=True
        ).astype(jnp.float32),
    )
    d_shared_out = grad_y.astype(jnp.bfloat16)
    d_sdown = matrix_product(shared_act.T, d_shared_out)
    d_shared_act = matrix_product(d_shared_out, sdown_full.T)
    d_sgate_val, d_sup_val = swish_gradients(d_shared_act, shared_gate_val, shared_up_val)
    d_sgate = matrix_product(h_ffn.T, d_sgate_val)
    d_sup = matrix_product(h_ffn.T, d_sup_val)
    d_h_ffn = (
        d_h_ffn + matrix_product(d_sgate_val, sgate_full.T) + matrix_product(d_sup_val, sup_full.T)
    )
    d_router = jnp.dot(h_ffn.astype(jnp.float32).T, d_logits, precision=lax.Precision.HIGHEST)
    d_h_ffn = d_h_ffn + jnp.dot(
        d_logits, router_full.astype(jnp.float32).T, precision=lax.Precision.HIGHEST
    )
    d_mid_norm, d_g_ffn = norm_back(middle, feedforward_gain, d_h_ffn)
    grad_mid = grad_y + d_mid_norm
    gffn_grad, router_grad, sgate_grad, sup_grad, sdown_grad = (
        lax.psum_scatter(d_g_ffn, ("ctx", "fsdp"), scatter_dimension=0, tiled=True),
        lax.psum_scatter(d_router, ("ctx", "fsdp"), scatter_dimension=0, tiled=True),
        lax.psum_scatter(d_sgate, ("ctx", "fsdp"), scatter_dimension=0, tiled=True),
        lax.psum_scatter(d_sup, ("ctx", "fsdp"), scatter_dimension=0, tiled=True),
        lax.psum_scatter(d_sdown, ("ctx", "fsdp"), scatter_dimension=0, tiled=True),
    )
    d_attn_out = grad_mid.astype(jnp.bfloat16)
    d_wo = matrix_product(attended.T, d_attn_out)
    d_attended = matrix_product(d_attn_out, wo_full.T).astype(jnp.bfloat16)
    d_attended_heads = jnp.transpose(d_attended.reshape(tok_count, HEADS, VDIM), (1, 0, 2))

    def head_backward(items):
        query_h, nope_h, value_h, dout_h, lse_h = items
        scores, keys = head_scores(query_h, nope_h)
        probs = jnp.exp(scores - lse_h[:, None])
        d_value = matrix_product(probs.astype(jnp.bfloat16).T, dout_h)
        d_probs = matrix_product(dout_h, value_h.T)
        delta = jnp.sum(probs * d_probs, axis=-1, keepdims=True)
        d_scores = (probs * (d_probs - delta)).astype(jnp.bfloat16)
        d_query = matrix_product(d_scores, keys) * softmax_scale
        d_keys = matrix_product(d_scores.T, query_h) * softmax_scale
        return (d_query, d_keys[:, :NOPE], d_keys[:, NOPE:], d_value)

    d_query_heads, d_nope_heads, d_rope_heads, d_value_heads = lax.map(
        head_backward, (query_heads, nope_heads, value_heads, d_attended_heads, lse_heads)
    )
    d_expand_part = (
        jnp.transpose(jnp.concatenate([d_nope_heads, d_value_heads], axis=-1), (1, 0, 2))
        .reshape(seq_total, HEADS * (NOPE + VDIM))
        .astype(jnp.bfloat16)
    )
    d_rope_all = jnp.sum(d_rope_heads, axis=0)
    d_wkvb = matrix_product(latent_all.T, d_expand_part)
    d_latent_part = matrix_product(d_expand_part, wkvb_full.T)
    d_latent, d_rope = (
        lax.psum_scatter(
            d_latent_part.astype(jnp.bfloat16), "ctx", scatter_dimension=0, tiled=True
        ).astype(jnp.float32),
        lax.psum_scatter(
            d_rope_all.astype(jnp.bfloat16), "ctx", scatter_dimension=0, tiled=True
        ).astype(jnp.float32),
    )
    d_latent_raw, d_g_latent = norm_back(latent_raw, latent_gain, d_latent)
    d_rope_raw = rotate_back(d_rope, cosine, sine)
    d_latent_in = jnp.concatenate([d_latent_raw, d_rope_raw], axis=-1).astype(jnp.bfloat16)
    d_wkva = matrix_product(h_attn.T, d_latent_in)
    d_h_attn = matrix_product(d_latent_in, wkva_full.T)
    d_query = jnp.transpose(d_query_heads, (1, 0, 2))
    d_query_raw = jnp.concatenate(
        [
            d_query[..., :NOPE],
            rotate_back(d_query[..., NOPE:], cosine[:, None, :], sine[:, None, :]),
        ],
        axis=-1,
    )
    d_query_low = d_query_raw.reshape(tok_count, HEADS * (NOPE + ROPE)).astype(jnp.bfloat16)
    d_wq = matrix_product(h_attn.T, d_query_low)
    d_h_attn = d_h_attn + matrix_product(d_query_low, wq_full.T)
    d_in_norm, d_g_attn = norm_back(input_rows, attention_gain, d_h_attn)
    input_grad = (grad_mid + d_in_norm).astype(jnp.bfloat16)
    gattn_grad, wq_grad, wkva_grad, glatent_grad, wkvb_grad, wo_grad = (
        lax.psum_scatter(d_g_attn, ("ctx", "fsdp"), scatter_dimension=0, tiled=True),
        lax.psum_scatter(d_wq, ("ctx", "fsdp"), scatter_dimension=0, tiled=True),
        lax.psum_scatter(d_wkva, ("ctx", "fsdp"), scatter_dimension=0, tiled=True),
        lax.psum_scatter(d_g_latent, ("ctx", "fsdp"), scatter_dimension=0, tiled=True),
        lax.psum_scatter(d_wkvb, ("ctx", "fsdp"), scatter_dimension=0, tiled=True),
        lax.psum_scatter(d_wo, ("ctx", "fsdp"), scatter_dimension=0, tiled=True),
    )
    return (
        output[None],
        input_grad[None],
        gattn_grad,
        wq_grad,
        wkva_grad,
        glatent_grad,
        wkvb_grad,
        wo_grad,
        gffn_grad,
        router_grad,
        sgate_grad,
        sup_grad,
        sdown_grad,
        expert_gate_weight_gradient,
        expert_up_weight_gradient,
        expert_down_weight_gradient,
    )


ALL = ("y", "z", "x", "c")
PLANE = ("y", "x", "c")
FSDP = ("z", "x", "c")
BF = jnp.bfloat16
F32 = jnp.float32
PAIRS = 8
SEQ_BLOCKS = 2


def swap(value, axis):
    return lax.ppermute(value, axis, [(0, 1), (1, 0)])


def swap_zq(value):
    pairs = [(z * 4 + q, q * 4 + z) for z in range(4) for q in range(4)]
    return lax.ppermute(value, FSDP, pairs)


def spread(value, axes):
    return lax.all_to_all(value, axes, split_axis=0, concat_axis=0, tiled=True)


def shift_z(value, step):
    return lax.ppermute(value, "z", [(i, (i + step) % 4) for i in range(4)])


class Chain:
    def __init__(self, hops):
        self.hops = hops
        self.pending = next(hops)
        self.result = None
        self.ended = False

    def advance(self, arrived):
        if self.ended:
            return
        try:
            self.pending = self.hops.send(arrived)
        except StopIteration as stop:
            self.pending, self.result, self.ended = [], stop.value, True


def tick(values, *chains):
    values, arrived = lax.optimization_barrier((values, [chain.pending for chain in chains]))
    for chain, parts in zip(chains, arrived):
        chain.advance(parts)
    return values


def one_hop(*parts):
    return (yield list(parts))


def swap_both(value):
    return lax.ppermute(value, ("y", "x"), [(i, 3 - i) for i in range(4)])


def gather_hops(block, last=None):
    if last is None:
        near = yield [swap(block, "y"), swap(block, "x"), swap_both(block)]
        near = [block, *near]
        far = yield [swap(part, "c") for part in near]
        return near + far
    by_x, by_y = yield [swap(block, "x"), swap(block, "y")]
    (diag,) = yield [swap(by_x, "y") if last == "y" else swap(by_y, "x")]
    near = [block, by_y, by_x, diag]
    far = yield [swap(part, "c") for part in near]
    return near + far


def add(*parts):
    return sum(part.astype(F32) for part in parts)


def reduce_hops(parts, first):
    got = yield [swap(part, "c") for part in parts[4:]]
    diag = add(parts[3], got[3]).astype(BF)
    if first is None:
        came = yield [
            swap(add(parts[1], got[1]).astype(BF), "y"),
            swap(add(parts[2], got[2]).astype(BF), "x"),
            swap_both(diag),
        ]
        return add(parts[0], got[0], *came)
    if first == "y":
        (got_diag,) = yield [swap(diag, "y")]
        to_y = add(parts[1], got[1]).astype(BF)
        to_x = add(parts[2], got[2], got_diag).astype(BF)
    else:
        (got_diag,) = yield [swap(diag, "x")]
        to_x = add(parts[2], got[2]).astype(BF)
        to_y = add(parts[1], got[1], got_diag).astype(BF)
    got_x, got_y = yield [swap(to_x, "x"), swap(to_y, "y")]
    return add(parts[0], got[0], got_x, got_y)


def home_hops(parts, first, step):
    total = yield from reduce_hops(parts, first)
    if step:
        (total,) = yield [shift_z(total.astype(BF), -step)]
    return total


def at_plane(step):
    return (lax.axis_index("z") + step) % 4


def line_hops(value):
    ups = [(i, i + 1) for i in range(3)]
    downs = [(i + 1, i) for i in range(3)]
    up, down = [value], [value]
    for _ in range(3):
        came = yield [lax.ppermute(up[-1], "z", ups), lax.ppermute(down[-1], "z", downs)]
        up.append(came[0])
        down.append(came[1])
    result = jnp.zeros((4,) + value.shape, value.dtype)
    result = lax.dynamic_update_index_in_dim(result, value, at_plane(0), 0)
    for hop in range(1, 4):
        result = lax.dynamic_update_index_in_dim(
            result, up[hop] + down[4 - hop], at_plane(4 - hop), 0
        )
    return result


def direct_hops(value):
    came = yield [shift_z(value, step) for step in range(1, 4)]
    result = jnp.zeros((4,) + value.shape, value.dtype)
    result = lax.dynamic_update_index_in_dim(result, value, at_plane(0), 0)
    for step in range(1, 4):
        result = lax.dynamic_update_index_in_dim(result, came[step - 1], at_plane(4 - step), 0)
    return result


def sum_hops(value):
    came = [lax.dynamic_index_in_dim(value, at_plane(0), 0, keepdims=False)]
    for step in (1, 3, 2):
        part = lax.dynamic_index_in_dim(value, at_plane(step), 0, keepdims=False)
        came += yield [shift_z(part, step)]
    return add(*came).astype(BF)


def dot_nt(left, right):
    return lax.dot_general(left, right, (((1,), (1,)), ((), ())), preferred_element_type=F32)


def dot_tn(left, right):
    return lax.dot_general(left, right, (((0,), (0,)), ((), ())), preferred_element_type=F32)


LIMIT = 60 * 1024 * 1024
VMEM_SPEC = pl.BlockSpec(memory_space=pltpu.VMEM)
SMEM_SPEC = pl.BlockSpec(memory_space=pltpu.SMEM)
ANY_SPEC = pl.BlockSpec(memory_space=pl.ANY)
STEPS = (0, 1, 2, 3)
ROWS = 128
SEQ = 256


def columns(step, size):
    return pl.ds(pl.multiple_of(step * size, size), size)


def attention_probs(meta, seq, query, expand, ropes, head):
    count = query.shape[0]
    half = count // 2
    keys = jnp.concatenate(
        [expand[:, 256 * head : 256 * head + 128], ropes[:, 128 * head : 128 * head + 128]], axis=1
    )
    rows = lax.broadcasted_iota(jnp.int32, (count, count), 0)
    cols = lax.broadcasted_iota(jnp.int32, (count, count), 1)
    own = meta[4]
    row_pos = jnp.where(rows < half, rows + own * half, rows - half + (1 - own) * half)
    col_pos = jnp.where(cols < half, cols + own * half, cols - half + (1 - own) * half)
    allowed = (col_pos <= row_pos) & (col_pos < meta[seq])
    queries = jnp.concatenate(
        [query[:, 128 * head : 128 * head + 128], query[:, 256:384]], axis=1
    )
    scores = dot_nt(queries, keys) * (NOPE + ROPE) ** (-0.5)
    scores = jnp.where(allowed, scores, NEGATIVE_FILL)
    expo = jnp.exp(scores - jnp.max(scores, axis=-1, keepdims=True))
    probs = expo / jnp.sum(expo, axis=-1, keepdims=True)
    return probs, queries, keys


def attend_kernel(meta, *refs):
    tokens = refs[:8]
    gain, latent_gain, wq, wl, we, cos_ref, sin_ref = refs[8:15]
    h_ref, query_ref, latent_ref, rope_ref, expand_ref, attended_ref, raw_ref = refs[15:22]
    for block in range(8):
        value = tokens[block][...].astype(F32)
        inverse = lax.rsqrt(jnp.mean(value * value, axis=-1, keepdims=True) + EPSILON)
        h_ref[pl.ds(block * ROWS, ROWS), :] = (value * inverse * gain[...]).astype(BF)

    def sequence(seq, carry):
        rows = pl.ds(pl.multiple_of(seq * SEQ, SEQ), SEQ)
        h_seq = h_ref[rows, :]
        cosine, sine = cos_ref[...], sin_ref[...]
        raw = jnp.dot(h_seq, wq[...], preferred_element_type=F32)
        rope = raw[:, 256:]
        rope = rope * cosine + pltpu.roll(rope, 64, 1) * sine
        query = jnp.concatenate([raw[:, :256], rope], axis=1).astype(BF)
        query_ref[rows, :] = query
        latent_in = jnp.dot(h_seq, wl[...], preferred_element_type=F32)
        value = latent_in[:, :KVR]

        @pl.when(seq == 0)
        def _():
            raw_ref[...] = value[:ROWS]

        inverse = lax.rsqrt(jnp.mean(value * value, axis=-1, keepdims=True) + EPSILON)
        latent = (value * inverse * latent_gain[...]).astype(BF)
        latent_ref[rows, :] = latent
        ropes = []
        for head in range(2):
            key = latent_in[:, KVR + 128 * head : KVR + 128 * head + 128]
            ropes.append(key * cosine + pltpu.roll(key, 64, 1) * sine)
        ropes = jnp.concatenate(ropes, axis=1).astype(BF)
        rope_ref[rows, :] = ropes
        expand = jnp.dot(latent, we[...], preferred_element_type=F32).astype(BF)
        expand_ref[rows, :] = expand
        for head in range(2):
            probs, _, _ = attention_probs(meta, seq, query, expand, ropes, head)
            values = expand[:, 256 * head + 128 : 256 * head + 256]
            attended_ref[rows, 128 * head : 128 * head + 128] = jnp.dot(
                probs.astype(BF), values, preferred_element_type=F32
            ).astype(BF)
        return carry

    lax.fori_loop(0, 4, sequence, 0)


def project_kernel(attended_ref, wo, *outs):
    def project(step, carry):
        cols = columns(step, 256)
        part = jnp.dot(attended_ref[...], wo[:, cols], preferred_element_type=F32).astype(BF)
        for block in range(8):
            outs[block][:, cols] = part[block * ROWS : (block + 1) * ROWS]
        return carry

    lax.fori_loop(0, wo.shape[1] // 256, project, 0)


def project(attended, wo):
    width = wo.shape[1]
    return pl.pallas_call(
        project_kernel,
        in_specs=[VMEM_SPEC] * 2,
        out_specs=[VMEM_SPEC] * 8,
        out_shape=[jax.ShapeDtypeStruct((ROWS, width), BF)] * 8,
        compiler_params=pltpu.CompilerParams(vmem_limit_bytes=LIMIT),
        cost_estimate=pl.CostEstimate(
            flops=10**9, bytes_accessed=6 * 10**6, transcendentals=0
        ),
        name="project",
    )(attended, wo)


def attend(meta, tokens, gain, latent_gain, wq, wl, we, cosine, sine):
    width = wq.shape[0]
    shape = jax.ShapeDtypeStruct
    return pl.pallas_call(
        attend_kernel,
        in_specs=[SMEM_SPEC] + [VMEM_SPEC] * 15,
        out_specs=[VMEM_SPEC] * 7,
        out_shape=[
            shape((8 * ROWS, width), BF),
            shape((8 * ROWS, 384), BF),
            shape((8 * ROWS, KVR), BF),
            shape((8 * ROWS, 256), BF),
            shape((8 * ROWS, 512), BF),
            shape((8 * ROWS, 256), BF),
            shape((ROWS, KVR), F32),
        ],
        compiler_params=pltpu.CompilerParams(vmem_limit_bytes=LIMIT),
        cost_estimate=pl.CostEstimate(
            flops=14 * 10**9, bytes_accessed=24 * 10**6, transcendentals=10**6
        ),
        name="attend",
    )(meta, *tokens, gain[None], latent_gain[None], wq, wl, we, cosine, sine)


def attend_back_kernel(meta, *refs):
    douts = refs[:8]
    query_ref, rope_ref, expand_ref, wq, we, wo, cos_ref, sin_ref = refs[8:16]
    dq_ref, dkv_ref = refs[16:18]
    lows = refs[18:26]
    hats = refs[26:34]
    dout_ref, datt_ref, low_ref = refs[34:37]
    scale = (NOPE + ROPE) ** (-0.5)
    for block in range(8):
        dout_ref[pl.ds(block * ROWS, ROWS), :] = douts[block][...]
    datt_ref[...] = dot_nt(dout_ref[...], wo[...]).astype(BF)

    def sequence(seq, carry):
        rows = pl.ds(pl.multiple_of(seq * SEQ, SEQ), SEQ)
        cosine, sine = cos_ref[...], sin_ref[...]
        query, expand, ropes = query_ref[rows, :], expand_ref[rows, :], rope_ref[rows, :]
        lane = lax.broadcasted_iota(jnp.int32, (SEQ, 128), 1)
        first = (lane % 64) < 32
        dq_rope = jnp.zeros((SEQ, 128), F32)
        dk_rope = jnp.zeros((SEQ, 128), F32)
        for head in range(2):
            probs, queries, keys = attention_probs(meta, seq, query, expand, ropes, head)
            values = expand[:, 256 * head + 128 : 256 * head + 256]
            dout = datt_ref[rows, 128 * head : 128 * head + 128]
            d_value = dot_tn(probs.astype(BF), dout)
            d_probs = dot_nt(dout, values)
            delta = jnp.sum(probs * d_probs, axis=-1, keepdims=True)
            d_scores = (probs * (d_probs - delta)).astype(BF)
            d_query = jnp.dot(d_scores, keys, preferred_element_type=F32) * scale
            d_keys = dot_tn(d_scores, queries) * scale
            dq_ref[rows, 128 * head : 128 * head + 128] = d_query[:, :128].astype(BF)
            dq_rope = dq_rope + d_query[:, 128:]
            dk_rope = dk_rope + jnp.where(first == (head == 0), d_keys[:, 128:], 0.0)
            dkv_ref[rows, 256 * head : 256 * head + 128] = d_keys[:, :128].astype(BF)
            dkv_ref[rows, 256 * head + 128 : 256 * head + 256] = d_value.astype(BF)
        dq_rope = dq_rope * cosine - pltpu.roll(dq_rope, 64, 1) * sine
        dq_ref[rows, 256:384] = dq_rope.astype(BF)
        both = jnp.where(first, dk_rope + pltpu.roll(dk_rope, 96, 1), 0.0)
        low_ref[rows, :KVR] = dot_nt(dkv_ref[rows, :], we[...]).astype(BF)
        low_ref[rows, KVR:] = both.astype(BF)
        return carry

    lax.fori_loop(0, 4, sequence, 0)
    for block in range(8):
        lows[block][...] = low_ref[pl.ds(block * ROWS, ROWS), :]

    def project(step, carry):
        cols = columns(step, 256)
        part = dot_nt(dq_ref[...], wq[cols, :]).astype(BF)
        for block in range(8):
            hats[block][:, cols] = part[block * ROWS : (block + 1) * ROWS]
        return carry

    lax.fori_loop(0, wq.shape[0] // 256, project, 0)


def attend_back(meta, douts, query, ropes, expand, wq, we, wo, cosine, sine):
    width = wq.shape[0]
    shape = jax.ShapeDtypeStruct
    out = pl.pallas_call(
        attend_back_kernel,
        in_specs=[SMEM_SPEC] + [VMEM_SPEC] * 16,
        out_specs=[VMEM_SPEC] * 18,
        out_shape=[
            shape((8 * ROWS, 384), BF),
            shape((8 * ROWS, 512), BF),
        ]
        + [shape((ROWS, KVR + 128), BF)] * 8
        + [shape((ROWS, width), BF)] * 8,
        scratch_shapes=[
            pltpu.VMEM((8 * ROWS, width), BF),
            pltpu.VMEM((8 * ROWS, 256), BF),
            pltpu.VMEM((8 * ROWS, KVR + 128), BF),
        ],
        compiler_params=pltpu.CompilerParams(vmem_limit_bytes=LIMIT),
        cost_estimate=pl.CostEstimate(
            flops=14 * 10**9, bytes_accessed=24 * 10**6, transcendentals=10**6
        ),
        name="attend_back",
    )(meta, *douts, query, ropes, expand, wq, we, wo, cosine, sine)
    return out[:2], out[2:10], out[10:]


def taken_slots(slot_ref, index, block, cap):
    slots = lax.broadcasted_iota(jnp.int32, (cap, ROWS), 0).astype(F32)
    return slot_ref[pl.ds(index[block], 1), :] == slots


def ffn_kernel(index, *refs):
    tokens = refs[:8]
    grads = refs[8:16]
    slot_ref, wg, wu, wd, si, sd = refs[16:22]
    refs = refs[23:] if len(refs) == 48 else refs[22:]
    out_ref, rows_ref, grows_ref, aw_ref, dg_ref, du_ref, dsi_ref, dsd_ref = refs[:8]
    dhs = refs[8:16]
    h_ref, g_ref, part_ref, pair_ref, drow_ref, dslot_ref, put_ref, weight_ref, sems = refs[16:25]
    cap = rows_ref.shape[0] // 8
    width = g_ref.shape[1]
    copies = []
    for block in range(8):
        here = pl.ds(block * ROWS, ROWS)
        copies.append(pltpu.make_async_copy(tokens[block], h_ref.at[here, :], sems.at[block]))
        copies.append(pltpu.make_async_copy(grads[block], g_ref.at[here, :], sems.at[8 + block]))
    for copy in copies:
        copy.start()
    for copy in copies:
        copy.wait()
    lane = lax.broadcasted_iota(jnp.int32, (cap, ROWS), 1)
    mine = (lane < 48) & (lane % 16 == index[8])
    for block in range(8):
        here = pl.ds(block * ROWS, ROWS)
        inside = pl.ds(block * cap, cap)
        pick = taken_slots(slot_ref, index, block, cap).astype(F32)
        put_ref[here, :cap] = pick.T.astype(BF)
        pick = pick.astype(BF)
        picked = jnp.dot(pick, h_ref[here, :], preferred_element_type=F32)
        rows_ref[inside, :] = picked[:, :width].astype(BF)
        grows_ref[inside, :] = jnp.dot(pick, g_ref[here, :], preferred_element_type=F32).astype(BF)
        weight = jnp.sum(jnp.where(mine, picked[:, width:], 0.0), axis=1, keepdims=True)
        weight_ref[inside, :] = jnp.broadcast_to(weight, (cap, ROWS))
    weight = weight_ref[:, :1]
    d_slot = jnp.zeros((8 * cap, 1), F32)
    for step in range(wg.shape[1] // 256):
        cols = slice(step * 256, step * 256 + 256)
        gate = jnp.dot(rows_ref[...], wg[:, cols], preferred_element_type=F32)
        up = jnp.dot(rows_ref[...], wu[:, cols], preferred_element_type=F32)
        d_act = dot_nt(grows_ref[...], wd[cols, :])
        sigma = jax.nn.sigmoid(gate)
        act = gate * sigma * up
        d_slot = d_slot + jnp.sum(act * d_act, axis=1, keepdims=True)
        d_act = d_act * weight
        aw_ref[:, cols] = (act * weight).astype(BF)
        dg_ref[:, cols] = (d_act * up * sigma * (1.0 + gate * (1.0 - sigma))).astype(BF)
        du_ref[:, cols] = (d_act * gate * sigma).astype(BF)
    lane = lax.broadcasted_iota(jnp.int32, (8 * cap, ROWS), 1)
    high = d_slot.astype(BF).astype(F32)
    dslot_ref[...] = jnp.where(
        lane == index[8], high, jnp.where(lane == 64 + index[8], d_slot - high, 0.0)
    ).astype(BF)
    for block in range(8):
        here = pl.ds(block * ROWS, ROWS)
        dhs[block][:, width:] = jnp.dot(
            put_ref[here, :cap], dslot_ref[pl.ds(block * cap, cap), :], preferred_element_type=F32
        ).astype(BF)
    shared = jnp.dot(h_ref[:, :width], si[...], preferred_element_type=F32)
    d_act = dot_nt(g_ref[...], sd[...])
    gate, up = shared[:, :128], shared[:, 128:]
    sigma = jax.nn.sigmoid(gate)
    act = (gate * sigma * up).astype(BF)
    d_gate = d_act * up * sigma * (1.0 + gate * (1.0 - sigma))
    d_up = d_act * gate * sigma
    d_both = jnp.concatenate([d_gate, d_up], axis=1).astype(BF)
    turned = d_both.T
    act_turned = act.T

    def tile(step, carry):
        cols = columns(step, 256)
        pair_ref[...] = jnp.dot(aw_ref[...], wd[:, cols], preferred_element_type=F32).astype(BF)
        drow_ref[...] = (dot_nt(dg_ref[...], wg[cols, :]) + dot_nt(du_ref[...], wu[cols, :])).astype(
            BF
        )
        from_shared = jnp.dot(act, sd[:, cols], preferred_element_type=F32)
        back_shared = dot_nt(d_both, si[cols, :])
        for block in range(8):
            here = slice(block * ROWS, (block + 1) * ROWS)
            inside = slice(block * cap, (block + 1) * cap)
            put = put_ref[here, :cap]
            part_ref[here, cols] = (
                from_shared[here]
                + jnp.dot(put, pair_ref[inside, :], preferred_element_type=F32)
            ).astype(BF)
            dhs[block][:, cols] = (
                back_shared[here]
                + jnp.dot(put, drow_ref[inside, :], preferred_element_type=F32)
            ).astype(BF)
        dsi_ref[:, cols] = jnp.dot(turned, h_ref[:, cols], preferred_element_type=F32)
        dsd_ref[:, cols] = jnp.dot(act_turned, g_ref[:, cols], preferred_element_type=F32)
        return carry

    lax.fori_loop(0, width // 256, tile, 0)
    copies = []
    for block in range(8):
        here = pl.ds(block * ROWS, ROWS)
        there = pl.ds(pl.multiple_of(index[block] * ROWS, ROWS), ROWS)
        copies.append(
            pltpu.make_async_copy(part_ref.at[here, :], out_ref.at[there, :], sems.at[block])
        )
    for copy in copies:
        copy.start()
    for copy in copies:
        copy.wait()


def ffn(index, tokens, grads, slot_of, weights, out, cap):
    width = grads[0].shape[1]
    hidden = weights[0].shape[1]
    shape = jax.ShapeDtypeStruct
    alias = [] if out is None else [out]
    result = pl.pallas_call(
        ffn_kernel,
        in_specs=[SMEM_SPEC] + [ANY_SPEC] * 16 + [VMEM_SPEC] * 6 + [ANY_SPEC] * len(alias),
        out_specs=[ANY_SPEC] + [VMEM_SPEC] * 15,
        out_shape=[
            shape((32 * ROWS, width), BF),
            shape((8 * cap, width), BF),
            shape((8 * cap, width), BF),
            shape((8 * cap, hidden), BF),
            shape((8 * cap, hidden), BF),
            shape((8 * cap, hidden), BF),
            shape((256, width), F32),
            shape((128, width), F32),
        ]
        + [shape((ROWS, width + 128), BF)] * 8,
        scratch_shapes=[
            pltpu.VMEM((8 * ROWS, width + 128), BF),
            pltpu.VMEM((8 * ROWS, width), BF),
            pltpu.VMEM((8 * ROWS, width), BF),
            pltpu.VMEM((8 * cap, 256), BF),
            pltpu.VMEM((8 * cap, 256), BF),
            pltpu.VMEM((8 * cap, ROWS), BF),
            pltpu.VMEM((8 * ROWS, ROWS), BF),
            pltpu.VMEM((8 * cap, ROWS), F32),
            pltpu.SemaphoreType.DMA((16,)),
        ],
        input_output_aliases={23: 0} if alias else {},
        compiler_params=pltpu.CompilerParams(vmem_limit_bytes=LIMIT),
        cost_estimate=pl.CostEstimate(
            flops=20 * 10**9, bytes_accessed=40 * 10**6, transcendentals=10**6
        ),
        name="ffn",
    )(index, *tokens, *grads, slot_of, *weights, *alias)
    return result[0], result[1:8], result[8:]


def rows_grad_kernel(left_ref, *refs):
    out_ref = refs[8]
    turned = left_ref[...].T
    total = jnp.zeros(out_ref.shape, F32)
    for block in range(8):
        total = total + jnp.dot(
            turned[:, block * ROWS : (block + 1) * ROWS],
            refs[block][...],
            preferred_element_type=F32,
        )
    out_ref[...] = total.astype(BF)


def rows_grad(left, blocks):
    width = blocks[0].shape[1]
    return pl.pallas_call(
        rows_grad_kernel,
        grid=(width // 512,),
        in_specs=[pl.BlockSpec(left.shape, lambda t: (0, 0))]
        + [pl.BlockSpec((ROWS, 512), lambda t: (0, t))] * 8,
        out_specs=pl.BlockSpec((left.shape[1], 512), lambda t: (0, t)),
        out_shape=jax.ShapeDtypeStruct((left.shape[1], width), BF),
        compiler_params=pltpu.CompilerParams(vmem_limit_bytes=LIMIT),
        cost_estimate=pl.CostEstimate(
            flops=10**9, bytes_accessed=6 * 10**6, transcendentals=0
        ),
        name="rows_grad",
    )(left, *blocks)


def local_tokens(
    tokens,
    attn_norm,
    w_query,
    w_latent,
    latent_norm,
    w_expand,
    w_output,
    ffn_norm,
    w_router,
    shared_gate,
    shared_up,
    shared_down,
    expert_gate,
    expert_up,
    expert_down,
    out_grad,
    seq_length,
    expert_ids,
    fill_order,
):
    tok = tokens.shape[1]
    width = tokens.shape[2]
    n_dev = 32
    n_experts = 16
    n_blocks = n_dev
    capacity = tok * TOPK // n_experts
    pair_count = tok * TOPK
    my_y = lax.axis_index("y")
    my_x = lax.axis_index("x")
    my_c = lax.axis_index("c")
    my_z = lax.axis_index("z")
    own_tokens = tokens[0]
    input_rows = own_tokens.astype(F32)

    route_ids = expert_ids[0]
    flat_ids = route_ids.reshape(pair_count)
    ranks = slot_rank(flat_ids, fill_order[0]).reshape(tok, TOPK)
    kept = ranks < capacity
    same = route_ids[:, :, None] == jnp.arange(n_experts, dtype=jnp.int32)[None, None, :]
    slot_plus = jnp.sum(
        jnp.where(same & kept[:, :, None], ranks[:, :, None] + 1, 0), axis=1
    )
    slot_table = (slot_plus - 1).astype(BF)

    n_small = [tok, attn_norm.shape[0], ffn_norm.shape[0], latent_norm.shape[0], 16, w_router.size]
    small_all = jnp.concatenate(
        [
            attn_norm,
            ffn_norm,
            latent_norm,
            jnp.broadcast_to(seq_length.astype(BF), (16,)),
            w_router.reshape(-1),
        ]
    )
    to_each = jnp.concatenate(
        [
            jnp.concatenate([slot_table.T, slot_table.T], axis=0),
            jnp.broadcast_to(small_all[None], (n_dev, small_all.shape[0])),
        ],
        axis=1,
    )

    def column_tiles(value, groups):
        rows = value.shape[0]
        view = jnp.transpose(value.reshape(rows, -1, ROWS), (1, 0, 2))
        return view.reshape(groups, -1, ROWS)

    def natural_rows(value, rows):
        view = value.reshape(4, 2, 4, -1, rows, ROWS)
        view = jnp.transpose(view, (1, 0, 2, 4, 3, 5))
        return view.reshape(n_dev * rows, -1)

    query_rows = w_query.shape[0] * 3
    packed = jnp.concatenate([column_tiles(w_query, PAIRS), column_tiles(w_expand, PAIRS)], axis=1)
    wl_all = lax.all_gather(w_latent, ALL, axis=0, tiled=True)
    valid = (my_y * tok + jnp.arange(tok, dtype=jnp.int32) < seq_length[0]).astype(F32)
    grad_y = out_grad[0].astype(F32) * valid[:, None]
    grad_low = grad_y.astype(BF)
    n_shared = shared_down.shape[0]
    shared_pad = 128 - n_shared
    n_half = expert_down.shape[1]
    half_pad = -n_half % 256

    def widen_columns(value, amount):
        return jnp.pad(value, ((0, 0), (0, amount)))

    own_low = own_tokens
    tokens_go = Chain(gather_hops(own_low, "y"))
    below_go = Chain(one_hop(shift_z(grad_low, 1)))
    packed = spread(packed, PLANE)
    packed, grad_low, w_output = tick((packed, grad_low, w_output), tokens_go, below_go)
    packed_go = Chain(line_hops(packed))
    zq_go = Chain(one_hop(swap_zq(w_output)))
    small = spread(to_each, ALL)
    grad_low, small = tick((grad_low, small), tokens_go, packed_go)
    grads_go = [Chain(gather_hops(grad_low, "x"))]
    grad_low, expert_gate, wl_all = tick(
        (grad_low, expert_gate, wl_all), tokens_go, packed_go, zq_go, grads_go[0]
    )

    def halves(value):
        first, second = value[0, :, :n_half], value[0, :, n_half:]
        mine = jnp.where(my_y == 0, first, second)
        return mine, Chain(one_hop(swap(jnp.where(my_y == 0, second, first), "y")))

    def whole_rows(mine, chain):
        other = chain.result[0]
        both = jnp.concatenate(
            [jnp.where(my_y == 0, mine, other), jnp.where(my_y == 0, other, mine)], axis=0
        )
        return widen_columns(both, half_pad)

    gate_mine, gate_go = halves(expert_gate)
    grads_go.append(Chain(gather_hops(below_go.result[0], "y")))
    latent_at = jnp.arange(KVR + 256)
    lane = (latent_at - KVR) % 128
    head = (latent_at - KVR) // 128
    latent_from = jnp.where(
        latent_at < KVR,
        latent_at,
        jnp.where(lane // 32 % 2 == head, KVR + lane % 32 + lane // 64 * 32, -1),
    )
    widen = (jnp.arange(KVR + ROPE)[:, None] == latent_from[None, :]).astype(BF)
    wl = matrix_product(wl_all, widen).astype(BF)
    grad_low, wl = tick((grad_low, wl), packed_go, grads_go[0], grads_go[1])

    cuts = [sum(n_small[: i + 1]) for i in range(len(n_small))]
    slot_of = small[:, : cuts[0]].astype(F32)
    attention_gain = small[:, cuts[0] : cuts[1]].reshape(-1).astype(F32)
    feedforward_gain = small[:, cuts[1] : cuts[2]].reshape(-1).astype(F32)
    latent_gain = small[:, cuts[2] : cuts[3]].reshape(-1).astype(F32)
    lengths = small[:16, cuts[3]].astype(jnp.int32)
    router = small[:, cuts[4] : cuts[5]].reshape(width, n_experts)
    packed = packed_go.result
    wq = natural_rows(packed[:, :, :query_rows], w_query.shape[0])
    we = natural_rows(packed[:, :, query_rows:], w_expand.shape[0])
    target = jnp.arange(384)
    rope_at = target - 256
    source = jnp.where(
        target < 256,
        target % 128 + target // 128 * 192,
        128 + rope_at % 32 + rope_at // 32 % 2 * 192 + rope_at // 64 * 32,
    )
    reorder = (jnp.arange(384)[:, None] == source[None, :]).astype(BF)
    wq = matrix_product(wq, reorder).astype(BF)
    half_pos = jnp.arange(tok, dtype=jnp.int32)
    pos_own = my_y * tok + half_pos
    cos_own, sin_own = rope_tables(pos_own, ROPE)
    cos_far, sin_far = rope_tables((1 - my_y) * tok + half_pos, ROPE)
    cos_pair = jnp.concatenate([jnp.concatenate([cos_own, cos_far], axis=0)] * 4, axis=1)
    sin_pair = jnp.concatenate([sin_own, sin_far], axis=0)
    sin_pair = jnp.concatenate([-sin_pair, -sin_pair, sin_pair, sin_pair], axis=1)
    my_seq = my_z * 4 + my_x * 2 + my_c
    meta = jnp.stack(
        [
            lengths[my_seq],
            lengths[my_z * 4 + (1 - my_x) * 2 + my_c],
            lengths[my_z * 4 + my_x * 2 + (1 - my_c)],
            lengths[my_z * 4 + (1 - my_x) * 2 + (1 - my_c)],
            my_y.astype(jnp.int32),
        ]
    )
    above_go = Chain(one_hop(shift_z(grad_low, -1)))
    wq, wl, we, meta, grad_low, expert_up = tick(
        (wq, wl, we, meta, grad_low, expert_up), grads_go[0], grads_go[1], above_go
    )

    wo_go = Chain(direct_hops(zq_go.result[0]))
    grads_go.append(Chain(gather_hops(above_go.result[0], "x")))
    up_mine, up_go = halves(expert_up)
    kept_values = attend(
        meta, tokens_go.result, attention_gain, latent_gain, wq, wl, we, cos_pair, sin_pair
    )
    kept_values, grad_low, shared_gate, shared_up = tick(
        (kept_values, grad_low, shared_gate, shared_up), wo_go, grads_go[1], grads_go[2], gate_go
    )
    h_attn, query, latent, ropes, expand, attended, latent_raw = kept_values
    wo = wo_go.result.reshape(2 * VDIM, width)
    attended_parts = project(attended, wo)

    def hidden_columns(value):
        return jnp.transpose(value.reshape(value.shape[0], n_dev, n_shared), (1, 0, 2))

    attended_parts = tick(attended_parts, grads_go[2])
    middle_go = Chain(reduce_hops(attended_parts, "y"))
    across_go = Chain(one_hop(shift_z(grad_low, 2)))
    tick((), middle_go)
    tick((), middle_go, grads_go[2])
    tick((), middle_go, across_go)
    grads_go.append(Chain(gather_hops(across_go.result[0], "y")))
    middle = input_rows + middle_go.result

    h_ffn = rms_norm(middle, feedforward_gain).astype(BF)
    gates = jax.nn.softmax(matrix_product(h_ffn, router), axis=-1)
    gates_high = gates.astype(BF)
    gates_left = gates - gates_high.astype(F32)
    gates_middle = gates_left.astype(BF)
    gates_low = (gates_left - gates_middle.astype(F32)).astype(BF)
    gates_rest = jnp.zeros((tok, 128 - 3 * n_experts), BF)
    sent = jnp.concatenate([h_ffn, gates_high, gates_middle, gates_low, gates_rest], axis=1)

    sent, shared_gate, shared_up = tick((sent, shared_gate, shared_up), grads_go[3])
    shared_both = spread(
        jnp.concatenate([hidden_columns(shared_gate), hidden_columns(shared_up)], axis=2), ALL
    )
    go = [Chain(gather_hops(sent, "y"))]
    below_go = Chain(one_hop(shift_z(sent, 1)))
    gate_w = whole_rows(gate_mine, gate_go)
    down_w = jnp.pad(expert_down[0], ((0, half_pad), (0, 0)))
    sent, gate_w, down_w = tick((sent, gate_w, down_w), go[0], grads_go[3], below_go)
    across_go = Chain(one_hop(shift_z(sent, 2)))
    go.append(Chain(gather_hops(below_go.result[0], "x")))
    shared_out = jnp.pad(shared_down, ((0, shared_pad), (0, 0)))
    sent, shared_both, shared_out = tick(
        (sent, shared_both, shared_out), go[0], go[1], grads_go[3], up_go
    )
    above_go = Chain(one_hop(shift_z(sent, -1)))
    shared_both = shared_both.reshape(width, 2 * n_shared)
    shared_in = jnp.concatenate(
        [
            widen_columns(shared_both[:, :n_shared], shared_pad),
            widen_columns(shared_both[:, n_shared:], shared_pad),
        ],
        axis=1,
    )
    weights = (gate_w, whole_rows(up_mine, up_go), down_w, shared_in, shared_out)
    weights = tick(weights, go[0], go[1], across_go)
    go.append(Chain(gather_hops(across_go.result[0])))
    grads_go = [grads_go[0], grads_go[1], grads_go[3], grads_go[2]]

    plane = jnp.stack(
        [
            (my_y ^ dy) * 16 + (my_x ^ dx) * 2 + (my_c ^ dc)
            for dc in range(2)
            for dx in range(2)
            for dy in range(2)
        ]
    ).astype(jnp.int32)
    saved = []
    homes = []
    out_part = None
    for number in range(4):
        index = plane + (my_z - STEPS[number]) % 4 * 4
        index = jnp.concatenate([index, my_seq[None].astype(jnp.int32)])
        results = ffn(
            index, go[number].result, grads_go[number].result, slot_of, weights, out_part, capacity
        )
        more = [above_go] if number == 0 else []
        out_part, kept_here, d_h_parts, weights = tick(
            results + (weights,), *go[number + 1 :], *homes, *more
        )
        if number == 0:
            go.append(Chain(gather_hops(above_go.result[0])))
        saved.append(kept_here)
        homes.append(Chain(home_hops(d_h_parts, None, STEPS[number])))

    rows, grad_rows, act_weighted, d_gate_val, d_up_val = (
        jnp.concatenate([item[i] for item in saved], axis=0) for i in range(5)
    )

    def column_halves(left, right):
        value = dot_tn(left, right)[:, :n_half].astype(BF)
        first, second = value[: width // 2], value[width // 2 :]
        mine = jnp.where(my_y == 0, first, second)
        return mine, Chain(one_hop(swap(jnp.where(my_y == 0, second, first), "y")))

    def whole_columns(mine, chain):
        other = chain.result[0]
        return jnp.concatenate(
            [jnp.where(my_y == 0, mine, other), jnp.where(my_y == 0, other, mine)], axis=1
        ).astype(F32)

    rows, grad_rows = tick((rows, grad_rows), *homes)
    d_gate_mine, d_gate_go = column_halves(rows, d_gate_val)
    rows, d_gate_mine, grad_rows = tick((rows, d_gate_mine, grad_rows), *homes)
    d_up_mine, d_up_go = column_halves(rows, d_up_val)
    d_up_mine, grad_rows = tick((d_up_mine, grad_rows), *homes)
    d_shared_in = sum(item[5] for item in saved).astype(BF).T.reshape(n_dev, width // n_dev, 256)
    d_shared_in = jnp.concatenate(
        [d_shared_in[..., :n_shared], d_shared_in[..., 128 : 128 + n_shared]], axis=2
    )
    d_shared_down = sum(item[6] for item in saved)[:n_shared]
    d_h_ffn = add(*(home.result for home in homes))
    d_gates = d_h_ffn[:, width : width + n_experts] + d_h_ffn[:, width + 64 : width + 64 + n_experts]
    d_h_ffn = d_h_ffn[:, :width]

    d_logits = gates * (d_gates - jnp.sum(gates * d_gates, axis=-1, keepdims=True))
    d_h_ffn = d_h_ffn + jnp.dot(
        d_logits, router.astype(F32).T, precision=lax.Precision.HIGHEST
    )
    d_mid_norm, d_g_ffn = norm_back(middle, feedforward_gain, d_h_ffn)
    grad_mid = grad_y + d_mid_norm

    grad_mid = tick(grad_mid)
    douts_go = Chain(gather_hops(grad_mid.astype(BF), "y"))
    d_down_w = dot_tn(act_weighted, grad_rows)[:n_half]
    d_down_w = tick(d_down_w, douts_go)
    d_shared_in = tick(d_shared_in, douts_go)
    d_router = jnp.dot(h_ffn.astype(F32).T, d_logits, precision=lax.Precision.HIGHEST)
    d_router = tick(d_router, douts_go)
    d_wo = rows_grad(attended, douts_go.result)
    d_wo, out_part = tick((d_wo, out_part))
    wo_go = Chain(sum_hops(d_wo.reshape(4, -1, width)))
    output = lax.psum_scatter(out_part, ALL, scatter_dimension=0, tiled=True)
    (d_query, d_expand), low_parts, hat_parts = tick(
        attend_back(
            meta, douts_go.result, query, ropes, expand, wq, we, wo, cos_pair, sin_pair
        ),
        wo_go,
    )

    def by_owner(value, rows_each):
        view = value.astype(BF).reshape(2, 4, 4, rows_each, -1, ROWS)
        return jnp.transpose(view, (1, 0, 2, 4, 3, 5)).reshape(4, 8, -1, ROWS)

    low_go = Chain(reduce_hops(low_parts, "x"))
    hat_go = Chain(reduce_hops(hat_parts, "y"))
    d_query = dot_nt(d_query, reorder).astype(BF)
    d_packed = jnp.concatenate(
        [
            by_owner(dot_tn(h_attn, d_query), w_query.shape[0]),
            by_owner(dot_tn(latent, d_expand), w_expand.shape[0]),
        ],
        axis=2,
    )
    d_packed = tick(d_packed, low_go, hat_go, wo_go)
    packed_go = Chain(sum_hops(d_packed))
    tick((), low_go, hat_go, wo_go)
    tick((), low_go, packed_go)
    d_low = low_go.result
    d_latent_raw, d_g_latent = norm_back(latent_raw, latent_gain, d_low[:, :KVR])
    d_rope = jnp.concatenate([d_low[:, KVR : KVR + 32], d_low[:, KVR + 64 : KVR + 96]], axis=1)
    d_rope_raw = rotate_back(d_rope, cos_own, sin_own)
    d_latent_in = jnp.concatenate([d_latent_raw, d_rope_raw], axis=-1).astype(BF)
    d_latent_in = tick(d_latent_in, hat_go, packed_go)
    dlat_go = Chain(gather_hops(d_latent_in, "x"))
    d_hattn = hat_go.result + dot_nt(d_latent_in, wl_all)
    d_in_norm, d_g_attn = norm_back(input_rows, attention_gain, d_hattn)
    input_grad = (grad_mid + d_in_norm).astype(BF)
    early = jnp.concatenate([d_g_ffn.reshape(n_dev, -1), d_router.reshape(n_dev, -1)], axis=1)
    small_grads = jnp.concatenate(
        [early, d_g_attn.reshape(n_dev, -1), d_g_latent.reshape(n_dev, -1)], axis=1
    )
    input_grad, small_grads = tick((input_grad, small_grads), dlat_go)
    tick((), dlat_go)
    tick((), dlat_go, zq_back := Chain(one_hop(swap_zq(wo_go.result))))
    my_pair = my_y * 4 + my_x * 2 + my_c
    part_cols = w_latent.shape[1] // PAIRS
    plane_dlat = jnp.concatenate(dlat_go.result, axis=0)
    d_columns = lax.dynamic_slice_in_dim(
        widen_columns(plane_dlat, 64), my_pair * part_cols, ROWS, axis=1
    )
    latent_go = Chain(sum_hops(by_owner(dot_tn(h_attn, d_columns), w_latent.shape[0])))
    tick((), packed_go, latent_go)
    tick((), latent_go)
    tick((), latent_go, d_gate_go, d_up_go)
    d_packed = spread(
        jnp.concatenate([packed_go.result, latent_go.result], axis=1), PLANE
    ).astype(F32)
    split = w_query.shape[0] * 3
    wq_grad = jnp.transpose(
        d_packed[:, :split].reshape(PAIRS, 3, w_query.shape[0], ROWS), (2, 0, 1, 3)
    ).reshape(w_query.shape)
    we_grad = jnp.transpose(
        d_packed[:, split : -w_latent.shape[0]].reshape(PAIRS, 4, w_expand.shape[0], ROWS),
        (2, 0, 1, 3),
    ).reshape(w_expand.shape)
    wl_grad = jnp.transpose(
        d_packed[:, -w_latent.shape[0] :, :part_cols], (1, 0, 2)
    ).reshape(w_latent.shape)
    wo_grad = zq_back.result[0].astype(F32)
    d_shared_in = spread(d_shared_in, ALL).astype(F32)

    def shared_columns(value):
        return jnp.transpose(value, (1, 0, 2)).reshape(width // n_dev, n_dev * n_shared)

    d_shared_gate = shared_columns(d_shared_in[..., :n_shared])
    d_shared_up = shared_columns(d_shared_in[..., n_shared:])
    d_expert_gate = whole_columns(d_gate_mine, d_gate_go)
    d_expert_up = whole_columns(d_up_mine, d_up_go)
    output = (middle + output.astype(F32)).astype(BF)
    small_grads = jnp.sum(spread(small_grads, ALL), axis=0)
    rows_each = width // n_dev
    gffn_grad = small_grads[:rows_each]
    router_grad = small_grads[rows_each : rows_each * (1 + n_experts)].reshape(rows_each, n_experts)
    late = small_grads[rows_each * (1 + n_experts) :]
    return (
        output[None],
        input_grad[None],
        late[: width // n_dev],
        wq_grad,
        wl_grad,
        late[width // n_dev :],
        we_grad,
        wo_grad,
        gffn_grad,
        router_grad,
        d_shared_gate,
        d_shared_up,
        d_shared_down,
        d_expert_gate[None],
        d_expert_up[None],
        d_down_w[None],
    )


def tokens_plan(mesh):
    fine = Mesh(mesh.devices.reshape(2, 4, 2, 2), ALL)
    rows = P(FSDP, "y", None)
    vector = P(ALL)
    matrix = P(ALL, None)
    in_specs = (
        rows,
        vector,
        matrix,
        matrix,
        vector,
        matrix,
        matrix,
        vector,
        matrix,
        matrix,
        matrix,
        matrix,
        rows,
        rows,
        rows,
        rows,
        P(FSDP),
        rows,
        P(FSDP, "y"),
    )
    out_specs = (
        rows,
        rows,
        vector,
        matrix,
        matrix,
        vector,
        matrix,
        matrix,
        vector,
        matrix,
        matrix,
        matrix,
        matrix,
        rows,
        rows,
        rows,
    )
    return jax.shard_map(
        local_tokens, mesh=fine, in_specs=in_specs, out_specs=out_specs, check_vma=False
    )


def weights_plan(mesh):
    in_specs = (
        P("fsdp", "ctx", None),
        P(("ctx", "fsdp")),
        P(("ctx", "fsdp"), None),
        P(("ctx", "fsdp"), None),
        P(("ctx", "fsdp")),
        P(("ctx", "fsdp"), None),
        P(("ctx", "fsdp"), None),
        P(("ctx", "fsdp")),
        P(("ctx", "fsdp"), None),
        P(("ctx", "fsdp"), None),
        P(("ctx", "fsdp"), None),
        P(("ctx", "fsdp"), None),
        P("fsdp", "ctx", None),
        P("fsdp", "ctx", None),
        P("fsdp", "ctx", None),
        P("fsdp", "ctx", None),
        P("fsdp"),
        P("fsdp", "ctx", None),
        P("fsdp", "ctx"),
    )
    out_specs = (
        P("fsdp", "ctx", None),
        P("fsdp", "ctx", None),
        P(("ctx", "fsdp")),
        P(("ctx", "fsdp"), None),
        P(("ctx", "fsdp"), None),
        P(("ctx", "fsdp")),
        P(("ctx", "fsdp"), None),
        P(("ctx", "fsdp"), None),
        P(("ctx", "fsdp")),
        P(("ctx", "fsdp"), None),
        P(("ctx", "fsdp"), None),
        P(("ctx", "fsdp"), None),
        P(("ctx", "fsdp"), None),
        P("fsdp", "ctx", None),
        P("fsdp", "ctx", None),
        P("fsdp", "ctx", None),
    )
    return jax.shard_map(local_weights, mesh=mesh, in_specs=in_specs, out_specs=out_specs, check_vma=False)


def solution(mesh):
    if mesh.shape["ctx"] == 2 and mesh.shape["fsdp"] == 16:
        return tokens_plan(mesh)
    return weights_plan(mesh)
```

```python
import jax
import jax.numpy as jnp
from jax import lax
from jax.experimental import pallas as pl
from jax.experimental.pallas import tpu as pltpu
from jax.sharding import Mesh
from jax.sharding import PartitionSpec as P

HEADS = 16
NOPE = 128
ROPE = 64
VDIM = 128
KVR = 512
TOPK = 6


EPSILON = 1e-06
ROPE_BASE = 10000.0
NEGATIVE_FILL = -1e30


def matrix_product(left, right):
    return jnp.dot(left, right, preferred_element_type=jnp.float32)


def rms_norm(values, gain):
    return values * lax.rsqrt(jnp.mean(values * values, axis=-1, keepdims=True) + EPSILON) * gain


def norm_back(values, gain, grad_out):
    inverse = lax.rsqrt(jnp.mean(values * values, axis=-1, keepdims=True) + EPSILON)
    normed = values * inverse
    gain_grad = jnp.sum(grad_out * normed, axis=0)
    scaled = grad_out * gain
    input_grad = inverse * (scaled - normed * jnp.mean(scaled * normed, axis=-1, keepdims=True))
    return (input_grad, gain_grad)


def rope_tables(positions, width):
    half = width // 2
    freqs = ROPE_BASE ** (-jnp.arange(half, dtype=jnp.float32) / half)
    angles = positions.astype(jnp.float32)[:, None] * freqs[None, :]
    return (jnp.cos(angles), jnp.sin(angles))


def rotate(values, cosine, sine):
    half = values.shape[-1] // 2
    first = values[..., :half]
    second = values[..., half:]
    return jnp.concatenate(
        [first * cosine - second * sine, second * cosine + first * sine], axis=-1
    )


def rotate_back(grads, cosine, sine):
    half = grads.shape[-1] // 2
    first = grads[..., :half]
    second = grads[..., half:]
    return jnp.concatenate(
        [first * cosine + second * sine, second * cosine - first * sine], axis=-1
    )


def slot_rank(expert_flat, priority):
    same = (expert_flat[:, None] == expert_flat[None, :]) & (priority[None, :] < priority[:, None])
    return jnp.sum(same.astype(jnp.int32), axis=1)


def swish_gradients(d_act, gate_val, up_val):
    sigma = jax.nn.sigmoid(gate_val)
    d_gate = (d_act * up_val * sigma * (1.0 + gate_val * (1.0 - sigma))).astype(jnp.bfloat16)
    d_up = (d_act * gate_val * sigma).astype(jnp.bfloat16)
    return (d_gate, d_up)


def local_weights(
    tokens,
    attn_norm,
    w_query,
    w_latent,
    latent_norm,
    w_expand,
    w_output,
    ffn_norm,
    w_router,
    shared_gate,
    shared_up,
    shared_down,
    expert_gate,
    expert_up,
    expert_down,
    out_grad,
    seq_length,
    expert_ids,
    fill_order,
):
    input_rows = tokens[0].astype(jnp.float32)
    tok_count = input_rows.shape[0]
    width = input_rows.shape[1]
    n_experts = expert_gate.shape[0] * lax.axis_size("fsdp")
    capacity = tok_count * TOPK // n_experts
    pair_count = tok_count * TOPK
    softmax_scale = (NOPE + ROPE) ** (-0.5)
    positions = lax.axis_index("ctx") * tok_count + jnp.arange(tok_count, dtype=jnp.int32)
    seq_used = seq_length[0]
    valid = (positions < seq_used).astype(jnp.float32)
    cosine, sine = rope_tables(positions, ROPE)
    attention_gain, wq_full, wkva_full, latent_gain, wkvb_full, wo_full = (
        lax.all_gather(attn_norm, ("ctx", "fsdp"), axis=0, tiled=True),
        lax.all_gather(w_query, ("ctx", "fsdp"), axis=0, tiled=True),
        lax.all_gather(w_latent, ("ctx", "fsdp"), axis=0, tiled=True),
        lax.all_gather(latent_norm, ("ctx", "fsdp"), axis=0, tiled=True),
        lax.all_gather(w_expand, ("ctx", "fsdp"), axis=0, tiled=True),
        lax.all_gather(w_output, ("ctx", "fsdp"), axis=0, tiled=True),
    )
    attention_gain = attention_gain.astype(jnp.float32)
    latent_gain = latent_gain.astype(jnp.float32)
    h_attn = rms_norm(input_rows, attention_gain).astype(jnp.bfloat16)
    query_raw = matrix_product(h_attn, wq_full).reshape(tok_count, HEADS, NOPE + ROPE)
    query_rot = jnp.concatenate(
        [
            query_raw[..., :NOPE],
            rotate(query_raw[..., NOPE:], cosine[:, None, :], sine[:, None, :]),
        ],
        axis=-1,
    ).astype(jnp.bfloat16)
    latent_in = matrix_product(h_attn, wkva_full)
    latent_raw = latent_in[:, :KVR]
    latent = rms_norm(latent_raw, latent_gain).astype(jnp.bfloat16)
    key_rope = rotate(latent_in[:, KVR:], cosine, sine).astype(jnp.bfloat16)
    latent_all, rope_all = (
        lax.all_gather(latent, "ctx", axis=0, tiled=True),
        lax.all_gather(key_rope, "ctx", axis=0, tiled=True),
    )
    expand_all = matrix_product(latent_all, wkvb_full).astype(jnp.bfloat16)
    seq_total = expand_all.shape[0]
    expand_heads = jnp.transpose(expand_all.reshape(seq_total, HEADS, NOPE + VDIM), (1, 0, 2))
    nope_heads = expand_heads[..., :NOPE]
    value_heads = expand_heads[..., NOPE:]
    query_heads = jnp.transpose(query_rot, (1, 0, 2))
    key_pos = jnp.arange(seq_total, dtype=jnp.int32)
    allowed = (key_pos[None, :] <= positions[:, None]) & (key_pos[None, :] < seq_used)

    def head_scores(query_h, nope_h):
        keys = jnp.concatenate([nope_h, rope_all], axis=-1)
        scores = matrix_product(query_h, keys.T) * softmax_scale
        return (jnp.where(allowed, scores, NEGATIVE_FILL), keys)

    def head_forward(items):
        query_h, nope_h, value_h = items
        scores, keys = head_scores(query_h, nope_h)
        highest_score = jnp.max(scores, axis=-1, keepdims=True)
        expo = jnp.exp(scores - highest_score)
        total = jnp.sum(expo, axis=-1, keepdims=True)
        probs = (expo / total).astype(jnp.bfloat16)
        attended_h = matrix_product(probs, value_h).astype(jnp.bfloat16)
        return (attended_h, highest_score[:, 0] + jnp.log(total[:, 0]))

    attended_heads, lse_heads = lax.map(head_forward, (query_heads, nope_heads, value_heads))
    attended = jnp.transpose(attended_heads, (1, 0, 2)).reshape(tok_count, HEADS * VDIM)
    middle = input_rows + matrix_product(attended, wo_full)
    feedforward_gain, router_full, sgate_full, sup_full, sdown_full = (
        lax.all_gather(ffn_norm, ("ctx", "fsdp"), axis=0, tiled=True),
        lax.all_gather(w_router, ("ctx", "fsdp"), axis=0, tiled=True),
        lax.all_gather(shared_gate, ("ctx", "fsdp"), axis=0, tiled=True),
        lax.all_gather(shared_up, ("ctx", "fsdp"), axis=0, tiled=True),
        lax.all_gather(shared_down, ("ctx", "fsdp"), axis=0, tiled=True),
    )
    feedforward_gain = feedforward_gain.astype(jnp.float32)
    expert_gate_gathered, expert_up_gathered, expert_down_gathered = (
        lax.all_gather(expert_gate, "ctx", axis=1, tiled=True),
        lax.all_gather(expert_up, "ctx", axis=1, tiled=True),
        lax.all_gather(expert_down, "ctx", axis=1, tiled=True),
    )
    expert_gate_matrix = expert_gate_gathered[0]
    expert_up_matrix = expert_up_gathered[0]
    edown_w = expert_down_gathered[0]
    h_ffn = rms_norm(middle, feedforward_gain).astype(jnp.bfloat16)
    gates = jax.nn.softmax(matrix_product(h_ffn, router_full), axis=-1)
    route_ids = expert_ids[0]
    onehot = (
        route_ids[:, :, None] == jnp.arange(n_experts, dtype=jnp.int32)[None, None, :]
    ).astype(jnp.float32)
    chosen = jnp.einsum("tke,te->tk", onehot, gates, precision=lax.Precision.HIGHEST)
    shared_gate_val = matrix_product(h_ffn, sgate_full)
    shared_up_val = matrix_product(h_ffn, sup_full)
    shared_act = (jax.nn.silu(shared_gate_val) * shared_up_val).astype(jnp.bfloat16)
    shared_out = matrix_product(shared_act, sdown_full)
    flat_ids = route_ids.reshape(pair_count)
    ranks = slot_rank(flat_ids, fill_order[0])
    kept = ranks < capacity
    dest = jnp.where(kept, flat_ids * capacity + ranks, n_experts * capacity)
    pair_token = jnp.arange(pair_count) // TOPK
    slot_total = n_experts * capacity
    send_rows = (
        jnp.zeros((slot_total + 1, width), jnp.bfloat16)
        .at[dest]
        .set(h_ffn[pair_token])[:slot_total]
    )
    received = lax.all_to_all(
        send_rows.reshape(n_experts, capacity, width),
        "fsdp",
        split_axis=0,
        concat_axis=0,
        tiled=True,
    )
    token_rows = received.reshape(-1, width)
    expert_gate_value = matrix_product(token_rows, expert_gate_matrix)
    expert_up_value = matrix_product(token_rows, expert_up_matrix)
    expert_act = (jax.nn.silu(expert_gate_value) * expert_up_value).astype(jnp.bfloat16)
    expert_output = matrix_product(expert_act, edown_w).astype(jnp.bfloat16)
    returned = lax.all_to_all(
        expert_output.reshape(received.shape), "fsdp", split_axis=0, concat_axis=0, tiled=True
    ).reshape(slot_total, width)
    zero_row = jnp.zeros((1, width), jnp.bfloat16)
    pair_out = (
        jnp.concatenate([returned, zero_row], axis=0)[dest]
        .astype(jnp.float32)
        .reshape(tok_count, TOPK, width)
    )
    kept_pairs = kept.reshape(tok_count, TOPK).astype(jnp.float32)
    pair_weight = chosen * kept_pairs
    routed = jnp.einsum("tk,tkd->td", pair_weight, pair_out, precision=lax.Precision.HIGHEST)
    output = (middle + shared_out + routed).astype(jnp.bfloat16)
    grad_y = out_grad[0].astype(jnp.float32) * valid[:, None]
    d_chosen = jnp.sum(pair_out * grad_y[:, None, :], axis=-1) * kept_pairs
    d_gates = jnp.einsum("tk,tke->te", d_chosen, onehot, precision=lax.Precision.HIGHEST)
    d_logits = gates * (d_gates - jnp.sum(gates * d_gates, axis=-1, keepdims=True))
    pair_grad_rows = (
        (pair_weight[:, :, None] * grad_y[:, None, :])
        .reshape(pair_count, width)
        .astype(jnp.bfloat16)
    )
    send_grads = (
        jnp.zeros((slot_total + 1, width), jnp.bfloat16).at[dest].set(pair_grad_rows)[:slot_total]
    )
    grad_rows = lax.all_to_all(
        send_grads.reshape(n_experts, capacity, width),
        "fsdp",
        split_axis=0,
        concat_axis=0,
        tiled=True,
    ).reshape(-1, width)
    d_edown = matrix_product(expert_act.T, grad_rows)
    expert_activation_grad = matrix_product(grad_rows, edown_w.T)
    expert_gate_value_grad, expert_up_value_grad = swish_gradients(
        expert_activation_grad, expert_gate_value, expert_up_value
    )
    d_egate = matrix_product(token_rows.T, expert_gate_value_grad)
    expert_up_weight_grad = matrix_product(token_rows.T, expert_up_value_grad)
    row_gradients = (
        matrix_product(expert_gate_value_grad, expert_gate_matrix.T)
        + matrix_product(expert_up_value_grad, expert_up_matrix.T)
    ).astype(jnp.bfloat16)
    back_rows = lax.all_to_all(
        row_gradients.reshape(received.shape), "fsdp", split_axis=0, concat_axis=0, tiled=True
    ).reshape(slot_total, width)
    d_pairs = (
        jnp.concatenate([back_rows, zero_row], axis=0)[dest]
        .astype(jnp.float32)
        .reshape(tok_count, TOPK, width)
    )
    d_h_ffn = jnp.sum(d_pairs, axis=1)
    expert_gate_weight_gradient, expert_up_weight_gradient, expert_down_weight_gradient = (
        lax.psum_scatter(
            d_egate[None].astype(jnp.bfloat16), "ctx", scatter_dimension=1, tiled=True
        ).astype(jnp.float32),
        lax.psum_scatter(
            expert_up_weight_grad[None].astype(jnp.bfloat16), "ctx", scatter_dimension=1, tiled=True
        ).astype(jnp.float32),
        lax.psum_scatter(
            d_edown[None].astype(jnp.bfloat16), "ctx", scatter_dimension=1, tiled=True
        ).astype(jnp.float32),
    )
    d_shared_out = grad_y.astype(jnp.bfloat16)
    d_sdown = matrix_product(shared_act.T, d_shared_out)
    d_shared_act = matrix_product(d_shared_out, sdown_full.T)
    d_sgate_val, d_sup_val = swish_gradients(d_shared_act, shared_gate_val, shared_up_val)
    d_sgate = matrix_product(h_ffn.T, d_sgate_val)
    d_sup = matrix_product(h_ffn.T, d_sup_val)
    d_h_ffn = (
        d_h_ffn + matrix_product(d_sgate_val, sgate_full.T) + matrix_product(d_sup_val, sup_full.T)
    )
    d_router = jnp.dot(h_ffn.astype(jnp.float32).T, d_logits, precision=lax.Precision.HIGHEST)
    d_h_ffn = d_h_ffn + jnp.dot(
        d_logits, router_full.astype(jnp.float32).T, precision=lax.Precision.HIGHEST
    )
    d_mid_norm, d_g_ffn = norm_back(middle, feedforward_gain, d_h_ffn)
    grad_mid = grad_y + d_mid_norm
    gffn_grad, router_grad, sgate_grad, sup_grad, sdown_grad = (
        lax.psum_scatter(d_g_ffn, ("ctx", "fsdp"), scatter_dimension=0, tiled=True),
        lax.psum_scatter(d_router, ("ctx", "fsdp"), scatter_dimension=0, tiled=True),
        lax.psum_scatter(d_sgate, ("ctx", "fsdp"), scatter_dimension=0, tiled=True),
        lax.psum_scatter(d_sup, ("ctx", "fsdp"), scatter_dimension=0, tiled=True),
        lax.psum_scatter(d_sdown, ("ctx", "fsdp"), scatter_dimension=0, tiled=True),
    )
    d_attn_out = grad_mid.astype(jnp.bfloat16)
    d_wo = matrix_product(attended.T, d_attn_out)
    d_attended = matrix_product(d_attn_out, wo_full.T).astype(jnp.bfloat16)
    d_attended_heads = jnp.transpose(d_attended.reshape(tok_count, HEADS, VDIM), (1, 0, 2))

    def head_backward(items):
        query_h, nope_h, value_h, dout_h, lse_h = items
        scores, keys = head_scores(query_h, nope_h)
        probs = jnp.exp(scores - lse_h[:, None])
        d_value = matrix_product(probs.astype(jnp.bfloat16).T, dout_h)
        d_probs = matrix_product(dout_h, value_h.T)
        delta = jnp.sum(probs * d_probs, axis=-1, keepdims=True)
        d_scores = (probs * (d_probs - delta)).astype(jnp.bfloat16)
        d_query = matrix_product(d_scores, keys) * softmax_scale
        d_keys = matrix_product(d_scores.T, query_h) * softmax_scale
        return (d_query, d_keys[:, :NOPE], d_keys[:, NOPE:], d_value)

    d_query_heads, d_nope_heads, d_rope_heads, d_value_heads = lax.map(
        head_backward, (query_heads, nope_heads, value_heads, d_attended_heads, lse_heads)
    )
    d_expand_part = (
        jnp.transpose(jnp.concatenate([d_nope_heads, d_value_heads], axis=-1), (1, 0, 2))
        .reshape(seq_total, HEADS * (NOPE + VDIM))
        .astype(jnp.bfloat16)
    )
    d_rope_all = jnp.sum(d_rope_heads, axis=0)
    d_wkvb = matrix_product(latent_all.T, d_expand_part)
    d_latent_part = matrix_product(d_expand_part, wkvb_full.T)
    d_latent, d_rope = (
        lax.psum_scatter(
            d_latent_part.astype(jnp.bfloat16), "ctx", scatter_dimension=0, tiled=True
        ).astype(jnp.float32),
        lax.psum_scatter(
            d_rope_all.astype(jnp.bfloat16), "ctx", scatter_dimension=0, tiled=True
        ).astype(jnp.float32),
    )
    d_latent_raw, d_g_latent = norm_back(latent_raw, latent_gain, d_latent)
    d_rope_raw = rotate_back(d_rope, cosine, sine)
    d_latent_in = jnp.concatenate([d_latent_raw, d_rope_raw], axis=-1).astype(jnp.bfloat16)
    d_wkva = matrix_product(h_attn.T, d_latent_in)
    d_h_attn = matrix_product(d_latent_in, wkva_full.T)
    d_query = jnp.transpose(d_query_heads, (1, 0, 2))
    d_query_raw = jnp.concatenate(
        [
            d_query[..., :NOPE],
            rotate_back(d_query[..., NOPE:], cosine[:, None, :], sine[:, None, :]),
        ],
        axis=-1,
    )
    d_query_low = d_query_raw.reshape(tok_count, HEADS * (NOPE + ROPE)).astype(jnp.bfloat16)
    d_wq = matrix_product(h_attn.T, d_query_low)
    d_h_attn = d_h_attn + matrix_product(d_query_low, wq_full.T)
    d_in_norm, d_g_attn = norm_back(input_rows, attention_gain, d_h_attn)
    input_grad = (grad_mid + d_in_norm).astype(jnp.bfloat16)
    gattn_grad, wq_grad, wkva_grad, glatent_grad, wkvb_grad, wo_grad = (
        lax.psum_scatter(d_g_attn, ("ctx", "fsdp"), scatter_dimension=0, tiled=True),
        lax.psum_scatter(d_wq, ("ctx", "fsdp"), scatter_dimension=0, tiled=True),
        lax.psum_scatter(d_wkva, ("ctx", "fsdp"), scatter_dimension=0, tiled=True),
        lax.psum_scatter(d_g_latent, ("ctx", "fsdp"), scatter_dimension=0, tiled=True),
        lax.psum_scatter(d_wkvb, ("ctx", "fsdp"), scatter_dimension=0, tiled=True),
        lax.psum_scatter(d_wo, ("ctx", "fsdp"), scatter_dimension=0, tiled=True),
    )
    return (
        output[None],
        input_grad[None],
        gattn_grad,
        wq_grad,
        wkva_grad,
        glatent_grad,
        wkvb_grad,
        wo_grad,
        gffn_grad,
        router_grad,
        sgate_grad,
        sup_grad,
        sdown_grad,
        expert_gate_weight_gradient,
        expert_up_weight_gradient,
        expert_down_weight_gradient,
    )


ALL = ("y", "z", "x", "c")
PLANE = ("y", "x", "c")
FSDP = ("z", "x", "c")
BF = jnp.bfloat16
F32 = jnp.float32
PAIRS = 8
SEQ_BLOCKS = 2


def swap(value, axis):
    return lax.ppermute(value, axis, [(0, 1), (1, 0)])


def swap_zq(value):
    pairs = [(z * 4 + q, q * 4 + z) for z in range(4) for q in range(4)]
    return lax.ppermute(value, FSDP, pairs)


def spread(value, axes):
    return lax.all_to_all(value, axes, split_axis=0, concat_axis=0, tiled=True)


def shift_z(value, step):
    return lax.ppermute(value, "z", [(i, (i + step) % 4) for i in range(4)])


class Chain:
    def __init__(self, hops):
        self.hops = hops
        self.pending = next(hops)
        self.result = None
        self.ended = False

    def advance(self, arrived):
        if self.ended:
            return
        try:
            self.pending = self.hops.send(arrived)
        except StopIteration as stop:
            self.pending, self.result, self.ended = [], stop.value, True


def tick(values, *chains):
    values, arrived = lax.optimization_barrier((values, [chain.pending for chain in chains]))
    for chain, parts in zip(chains, arrived):
        chain.advance(parts)
    return values


def one_hop(*parts):
    return (yield list(parts))


def finish(chain):
    while not chain.ended:
        chain.advance(chain.pending)
    return chain.result


def run(hops):
    return finish(Chain(hops))


def gather_hops(block):
    (by_y,) = yield [swap(block, "y")]
    pair = jnp.concatenate([block, by_y], axis=0)
    (by_x,) = yield [swap(pair, "x")]
    near = jnp.concatenate([pair, by_x], axis=0)
    (far,) = yield [swap(near, "c")]
    return near, far


def add(*parts):
    return sum(part.astype(F32) for part in parts)


def reduce_hops(parts, links=("x", "y")):
    near, far = parts
    half = near.shape[0] // 2
    (got,) = yield [swap(far, "c")]
    pair = add(near[:half], got[:half])
    (got,) = yield [swap(add(near[half:], got[half:]).astype(BF), links[0])]
    pair = add(pair, got)
    (got,) = yield [swap(pair[half // 2 :].astype(BF), links[1])]
    return add(pair[: half // 2], got)


def home_hops(parts, step, links=("x", "y")):
    total = yield from reduce_hops(parts, links)
    if step:
        (total,) = yield [shift_z(total.astype(BF), -step)]
    return total


def at_plane(step):
    return (lax.axis_index("z") + step) % 4


def line_hops(value):
    ups = [(i, i + 1) for i in range(3)]
    downs = [(i + 1, i) for i in range(3)]
    up, down = [value], [value]
    for _ in range(3):
        came = yield [lax.ppermute(up[-1], "z", ups), lax.ppermute(down[-1], "z", downs)]
        up.append(came[0])
        down.append(came[1])
    result = jnp.zeros((4,) + value.shape, value.dtype)
    result = lax.dynamic_update_index_in_dim(result, value, at_plane(0), 0)
    for hop in range(1, 4):
        result = lax.dynamic_update_index_in_dim(
            result, up[hop] + down[4 - hop], at_plane(4 - hop), 0
        )
    return result


def direct_hops(value):
    came = yield [shift_z(value, step) for step in range(1, 4)]
    result = jnp.zeros((4,) + value.shape, value.dtype)
    result = lax.dynamic_update_index_in_dim(result, value, at_plane(0), 0)
    for step in range(1, 4):
        result = lax.dynamic_update_index_in_dim(result, came[step - 1], at_plane(4 - step), 0)
    return result


def sum_hops(value, at_once):
    came = [lax.dynamic_index_in_dim(value, at_plane(0), 0, keepdims=False)]
    for steps in ((1, 2, 3),) if at_once else ((1,), (3,), (2,)):
        came += yield [
            shift_z(lax.dynamic_index_in_dim(value, at_plane(step), 0, keepdims=False), step)
            for step in steps
        ]
    return add(*came).astype(BF)


def dot_nt(left, right):
    return lax.dot_general(left, right, (((1,), (1,)), ((), ())), preferred_element_type=F32)


def dot_tn(left, right):
    return lax.dot_general(left, right, (((0,), (0,)), ((), ())), preferred_element_type=F32)


LIMIT = 60 * 1024 * 1024
VMEM_SPEC = pl.BlockSpec(memory_space=pltpu.VMEM)
SMEM_SPEC = pl.BlockSpec(memory_space=pltpu.SMEM)
ANY_SPEC = pl.BlockSpec(memory_space=pl.ANY)
STEPS = (0, 1, 2, 3)
ROWS = 128
SEQ = 256


def columns(step, size):
    return pl.ds(pl.multiple_of(step * size, size), size)


def attention_probs(meta, seq, query, expand, ropes, head):
    count = query.shape[0]
    half = count // 2
    keys = jnp.concatenate(
        [expand[:, 256 * head : 256 * head + 128], ropes[:, 128 * head : 128 * head + 128]], axis=1
    )
    rows = lax.broadcasted_iota(jnp.int32, (count, count), 0)
    cols = lax.broadcasted_iota(jnp.int32, (count, count), 1)
    own = meta[4]
    row_pos = jnp.where(rows < half, rows + own * half, rows - half + (1 - own) * half)
    col_pos = jnp.where(cols < half, cols + own * half, cols - half + (1 - own) * half)
    allowed = (col_pos <= row_pos) & (col_pos < meta[seq])
    queries = jnp.concatenate(
        [query[:, 128 * head : 128 * head + 128], query[:, 256:384]], axis=1
    )
    scores = dot_nt(queries, keys) * (NOPE + ROPE) ** (-0.5)
    scores = jnp.where(allowed, scores, NEGATIVE_FILL)
    expo = jnp.exp(scores - jnp.max(scores, axis=-1, keepdims=True))
    probs = expo / jnp.sum(expo, axis=-1, keepdims=True)
    return probs, queries, keys


def attend_kernel(meta, *refs):
    tokens = refs[:2]
    gain, latent_gain, wq, wl, we, cos_ref, sin_ref = refs[2:9]
    h_ref, query_ref, latent_ref, rope_ref, expand_ref, attended_ref, raw_ref = refs[9:]
    for block in range(8):
        value = tokens[block // 4][pl.ds(block % 4 * ROWS, ROWS), :].astype(F32)
        inverse = lax.rsqrt(jnp.mean(value * value, axis=-1, keepdims=True) + EPSILON)
        h_ref[pl.ds(block * ROWS, ROWS), :] = (value * inverse * gain[...]).astype(BF)

    def sequence(seq, carry):
        rows = pl.ds(pl.multiple_of(seq * SEQ, SEQ), SEQ)
        h_seq = h_ref[rows, :]
        cosine, sine = cos_ref[...], sin_ref[...]
        raw = jnp.dot(h_seq, wq[...], preferred_element_type=F32)
        rope = raw[:, 256:]
        rope = rope * cosine + pltpu.roll(rope, 64, 1) * sine
        query = jnp.concatenate([raw[:, :256], rope], axis=1).astype(BF)
        query_ref[rows, :] = query
        latent_in = jnp.dot(h_seq, wl[...], preferred_element_type=F32)
        value = latent_in[:, :KVR]

        @pl.when(seq == 0)
        def _():
            raw_ref[...] = value[:ROWS]

        inverse = lax.rsqrt(jnp.mean(value * value, axis=-1, keepdims=True) + EPSILON)
        latent = (value * inverse * latent_gain[...]).astype(BF)
        latent_ref[rows, :] = latent
        ropes = []
        for head in range(2):
            key = latent_in[:, KVR + 128 * head : KVR + 128 * head + 128]
            ropes.append(key * cosine + pltpu.roll(key, 64, 1) * sine)
        ropes = jnp.concatenate(ropes, axis=1).astype(BF)
        rope_ref[rows, :] = ropes
        expand = jnp.dot(latent, we[...], preferred_element_type=F32).astype(BF)
        expand_ref[rows, :] = expand
        for head in range(2):
            probs, _, _ = attention_probs(meta, seq, query, expand, ropes, head)
            values = expand[:, 256 * head + 128 : 256 * head + 256]
            attended_ref[rows, 128 * head : 128 * head + 128] = jnp.dot(
                probs.astype(BF), values, preferred_element_type=F32
            ).astype(BF)
        return carry

    lax.fori_loop(0, 4, sequence, 0)


def project_kernel(attended_ref, wo, *outs):
    def project(step, carry):
        cols = columns(step, 256)
        part = jnp.dot(attended_ref[...], wo[:, cols], preferred_element_type=F32).astype(BF)
        outs[0][:, cols] = part[: 4 * ROWS]
        outs[1][:, cols] = part[4 * ROWS :]
        return carry

    lax.fori_loop(0, wo.shape[1] // 256, project, 0)


def project(attended, wo):
    width = wo.shape[1]
    return pl.pallas_call(
        project_kernel,
        in_specs=[VMEM_SPEC] * 2,
        out_specs=[VMEM_SPEC] * 2,
        out_shape=[jax.ShapeDtypeStruct((4 * ROWS, width), BF)] * 2,
        compiler_params=pltpu.CompilerParams(vmem_limit_bytes=LIMIT),
        cost_estimate=pl.CostEstimate(
            flops=10**9, bytes_accessed=6 * 10**6, transcendentals=0
        ),
        name="project",
    )(attended, wo)


def attend(meta, tokens, gain, latent_gain, wq, wl, we, cosine, sine):
    width = wq.shape[0]
    shape = jax.ShapeDtypeStruct
    return pl.pallas_call(
        attend_kernel,
        in_specs=[SMEM_SPEC] + [VMEM_SPEC] * 9,
        out_specs=[VMEM_SPEC] * 7,
        out_shape=[
            shape((8 * ROWS, width), BF),
            shape((8 * ROWS, 384), BF),
            shape((8 * ROWS, KVR), BF),
            shape((8 * ROWS, 256), BF),
            shape((8 * ROWS, 512), BF),
            shape((8 * ROWS, 256), BF),
            shape((ROWS, KVR), F32),
        ],
        compiler_params=pltpu.CompilerParams(vmem_limit_bytes=LIMIT),
        cost_estimate=pl.CostEstimate(
            flops=14 * 10**9, bytes_accessed=24 * 10**6, transcendentals=10**6
        ),
        name="attend",
    )(meta, *tokens, gain[None], latent_gain[None], wq, wl, we, cosine, sine)


def attend_back_kernel(meta, *refs):
    douts = refs[:2]
    query_ref, rope_ref, expand_ref, wq, we, wo, cos_ref, sin_ref = refs[2:10]
    dq_ref, dkv_ref = refs[10:12]
    lows = refs[12:14]
    hats = refs[14:16]
    datt_ref, low_ref = refs[16:]
    scale = (NOPE + ROPE) ** (-0.5)
    for side in range(2):
        rows = pl.ds(side * 4 * ROWS, 4 * ROWS)
        datt_ref[rows, :] = dot_nt(douts[side][...], wo[...]).astype(BF)

    def sequence(seq, carry):
        rows = pl.ds(pl.multiple_of(seq * SEQ, SEQ), SEQ)
        cosine, sine = cos_ref[...], sin_ref[...]
        query, expand, ropes = query_ref[rows, :], expand_ref[rows, :], rope_ref[rows, :]
        lane = lax.broadcasted_iota(jnp.int32, (SEQ, 128), 1)
        first = (lane % 64) < 32
        dq_rope = jnp.zeros((SEQ, 128), F32)
        dk_rope = jnp.zeros((SEQ, 128), F32)
        for head in range(2):
            probs, queries, keys = attention_probs(meta, seq, query, expand, ropes, head)
            values = expand[:, 256 * head + 128 : 256 * head + 256]
            dout = datt_ref[rows, 128 * head : 128 * head + 128]
            d_value = dot_tn(probs.astype(BF), dout)
            d_probs = dot_nt(dout, values)
            delta = jnp.sum(probs * d_probs, axis=-1, keepdims=True)
            d_scores = (probs * (d_probs - delta)).astype(BF)
            d_query = jnp.dot(d_scores, keys, preferred_element_type=F32) * scale
            d_keys = dot_tn(d_scores, queries) * scale
            dq_ref[rows, 128 * head : 128 * head + 128] = d_query[:, :128].astype(BF)
            dq_rope = dq_rope + d_query[:, 128:]
            dk_rope = dk_rope + jnp.where(first == (head == 0), d_keys[:, 128:], 0.0)
            dkv_ref[rows, 256 * head : 256 * head + 128] = d_keys[:, :128].astype(BF)
            dkv_ref[rows, 256 * head + 128 : 256 * head + 256] = d_value.astype(BF)
        dq_rope = dq_rope * cosine - pltpu.roll(dq_rope, 64, 1) * sine
        dq_ref[rows, 256:384] = dq_rope.astype(BF)
        both = jnp.where(first, dk_rope + pltpu.roll(dk_rope, 96, 1), 0.0)
        low_ref[rows, :KVR] = dot_nt(dkv_ref[rows, :], we[...]).astype(BF)
        low_ref[rows, KVR:] = both.astype(BF)
        return carry

    lax.fori_loop(0, 4, sequence, 0)
    for side in range(2):
        lows[side][...] = low_ref[pl.ds(side * 4 * ROWS, 4 * ROWS), :]

    def project(step, carry):
        cols = columns(step, 256)
        part = dot_nt(dq_ref[...], wq[cols, :]).astype(BF)
        hats[0][:, cols] = part[: 4 * ROWS]
        hats[1][:, cols] = part[4 * ROWS :]
        return carry

    lax.fori_loop(0, wq.shape[0] // 256, project, 0)


def attend_back(meta, douts, query, ropes, expand, wq, we, wo, cosine, sine):
    width = wq.shape[0]
    shape = jax.ShapeDtypeStruct
    out = pl.pallas_call(
        attend_back_kernel,
        in_specs=[SMEM_SPEC] + [VMEM_SPEC] * 10,
        out_specs=[VMEM_SPEC] * 6,
        out_shape=[
            shape((8 * ROWS, 384), BF),
            shape((8 * ROWS, 512), BF),
        ]
        + [shape((4 * ROWS, KVR + 128), BF)] * 2
        + [shape((4 * ROWS, width), BF)] * 2,
        scratch_shapes=[
            pltpu.VMEM((8 * ROWS, 256), BF),
            pltpu.VMEM((8 * ROWS, KVR + 128), BF),
        ],
        compiler_params=pltpu.CompilerParams(vmem_limit_bytes=LIMIT),
        cost_estimate=pl.CostEstimate(
            flops=14 * 10**9, bytes_accessed=24 * 10**6, transcendentals=10**6
        ),
        name="attend_back",
    )(meta, *douts, query, ropes, expand, wq, we, wo, cosine, sine)
    return out[:2], out[2:4], out[4:]


def taken_slots(slot_ref, index, block, cap):
    slots = lax.broadcasted_iota(jnp.int32, (cap, ROWS), 0).astype(F32)
    return slot_ref[pl.ds(index[block], 1), :] == slots


def ffn_kernel(index, *refs):
    tokens = refs[:2]
    grads = refs[2:4]
    slot_ref, wg, wu, wd, si, sd = refs[4:10]
    rows_ref, grows_ref, aw_ref, dg_ref, du_ref, dsi_ref, dsd_ref = refs[10:17]
    dhs = refs[17:19]
    outs = refs[19:21]
    h_ref, g_ref, pair_ref, drow_ref, dslot_ref, put_ref, weight_ref, sems = refs[21:]
    cap = rows_ref.shape[0] // 8
    width = g_ref.shape[1]
    copies = []
    for side in range(2):
        here = pl.ds(side * 4 * ROWS, 4 * ROWS)
        copies.append(pltpu.make_async_copy(tokens[side], h_ref.at[here, :], sems.at[side]))
        copies.append(pltpu.make_async_copy(grads[side], g_ref.at[here, :], sems.at[2 + side]))
    for copy in copies:
        copy.start()
    for copy in copies:
        copy.wait()
    lane = lax.broadcasted_iota(jnp.int32, (cap, ROWS), 1)
    mine = (lane < 48) & (lane % 16 == index[8])
    for block in range(8):
        here = pl.ds(block * ROWS, ROWS)
        inside = pl.ds(block * cap, cap)
        pick = taken_slots(slot_ref, index, block, cap).astype(F32)
        put_ref[here, :cap] = pick.T.astype(BF)
        pick = pick.astype(BF)
        picked = jnp.dot(pick, h_ref[here, :], preferred_element_type=F32)
        rows_ref[inside, :] = picked[:, :width].astype(BF)
        grows_ref[inside, :] = jnp.dot(pick, g_ref[here, :], preferred_element_type=F32).astype(BF)
        weight = jnp.sum(jnp.where(mine, picked[:, width:], 0.0), axis=1, keepdims=True)
        weight_ref[inside, :] = jnp.broadcast_to(weight, (cap, ROWS))
    weight = weight_ref[:, :1]
    d_slot = jnp.zeros((8 * cap, 1), F32)
    for step in range(wg.shape[1] // 256):
        cols = slice(step * 256, step * 256 + 256)
        gate = jnp.dot(rows_ref[...], wg[:, cols], preferred_element_type=F32)
        up = jnp.dot(rows_ref[...], wu[:, cols], preferred_element_type=F32)
        d_act = dot_nt(grows_ref[...], wd[cols, :])
        sigma = jax.nn.sigmoid(gate)
        act = gate * sigma * up
        d_slot = d_slot + jnp.sum(act * d_act, axis=1, keepdims=True)
        d_act = d_act * weight
        aw_ref[:, cols] = (act * weight).astype(BF)
        dg_ref[:, cols] = (d_act * up * sigma * (1.0 + gate * (1.0 - sigma))).astype(BF)
        du_ref[:, cols] = (d_act * gate * sigma).astype(BF)
    lane = lax.broadcasted_iota(jnp.int32, (8 * cap, ROWS), 1)
    high = d_slot.astype(BF).astype(F32)
    dslot_ref[...] = jnp.where(
        lane == index[8], high, jnp.where(lane == 64 + index[8], d_slot - high, 0.0)
    ).astype(BF)
    for block in range(8):
        here = pl.ds(block * ROWS, ROWS)
        dhs[block // 4][pl.ds(block % 4 * ROWS, ROWS), width:] = jnp.dot(
            put_ref[here, :cap], dslot_ref[pl.ds(block * cap, cap), :], preferred_element_type=F32
        ).astype(BF)
    shared = jnp.dot(h_ref[:, :width], si[...], preferred_element_type=F32)
    d_act = dot_nt(g_ref[...], sd[...])
    gate, up = shared[:, :128], shared[:, 128:]
    sigma = jax.nn.sigmoid(gate)
    act = (gate * sigma * up).astype(BF)
    d_gate = d_act * up * sigma * (1.0 + gate * (1.0 - sigma))
    d_up = d_act * gate * sigma
    d_both = jnp.concatenate([d_gate, d_up], axis=1).astype(BF)
    turned = d_both.T
    act_turned = act.T

    def tile(step, carry):
        cols = columns(step, 256)
        pair_ref[...] = jnp.dot(aw_ref[...], wd[:, cols], preferred_element_type=F32).astype(BF)
        drow_ref[...] = (dot_nt(dg_ref[...], wg[cols, :]) + dot_nt(du_ref[...], wu[cols, :])).astype(
            BF
        )
        from_shared = jnp.dot(act, sd[:, cols], preferred_element_type=F32)
        back_shared = dot_nt(d_both, si[cols, :])
        for block in range(8):
            here = slice(block * ROWS, (block + 1) * ROWS)
            inside = slice(block * cap, (block + 1) * cap)
            half = pl.ds(block % 4 * ROWS, ROWS)
            put = put_ref[here, :cap]
            place = pl.ds((0, 2, 1, 3)[block % 4] * ROWS, ROWS)
            outs[block // 4][place, cols] = (
                from_shared[here]
                + jnp.dot(put, pair_ref[inside, :], preferred_element_type=F32)
            ).astype(BF)
            dhs[block // 4][half, cols] = (
                back_shared[here]
                + jnp.dot(put, drow_ref[inside, :], preferred_element_type=F32)
            ).astype(BF)
        dsi_ref[:, cols] = jnp.dot(turned, h_ref[:, cols], preferred_element_type=F32)
        dsd_ref[:, cols] = jnp.dot(act_turned, g_ref[:, cols], preferred_element_type=F32)
        return carry

    lax.fori_loop(0, width // 256, tile, 0)


def ffn(index, tokens, grads, slot_of, weights, cap):
    width = grads[0].shape[1]
    hidden = weights[0].shape[1]
    shape = jax.ShapeDtypeStruct
    result = pl.pallas_call(
        ffn_kernel,
        in_specs=[SMEM_SPEC] + [ANY_SPEC] * 4 + [VMEM_SPEC] * 6,
        out_specs=[VMEM_SPEC] * 11,
        out_shape=[
            shape((8 * cap, width), BF),
            shape((8 * cap, width), BF),
            shape((8 * cap, hidden), BF),
            shape((8 * cap, hidden), BF),
            shape((8 * cap, hidden), BF),
            shape((256, width), F32),
            shape((128, width), F32),
        ]
        + [shape((4 * ROWS, width + 128), BF)] * 2
        + [shape((4 * ROWS, width), BF)] * 2,
        scratch_shapes=[
            pltpu.VMEM((8 * ROWS, width + 128), BF),
            pltpu.VMEM((8 * ROWS, width), BF),
            pltpu.VMEM((8 * cap, 256), BF),
            pltpu.VMEM((8 * cap, 256), BF),
            pltpu.VMEM((8 * cap, ROWS), BF),
            pltpu.VMEM((8 * ROWS, ROWS), BF),
            pltpu.VMEM((8 * cap, ROWS), F32),
            pltpu.SemaphoreType.DMA((4,)),
        ],
        compiler_params=pltpu.CompilerParams(vmem_limit_bytes=LIMIT),
        cost_estimate=pl.CostEstimate(
            flops=20 * 10**9, bytes_accessed=40 * 10**6, transcendentals=10**6
        ),
        name="ffn",
    )(index, *tokens, *grads, slot_of, *weights)
    return result[:7], result[7:9], result[9:]


def rows_grad_kernel(left_ref, near_ref, far_ref, out_ref):
    turned = left_ref[...].T
    half = near_ref.shape[0]
    out_ref[...] = (
        jnp.dot(turned[:, :half], near_ref[...], preferred_element_type=F32)
        + jnp.dot(turned[:, half:], far_ref[...], preferred_element_type=F32)
    ).astype(BF)


def rows_grad(left, rows):
    width = rows[0].shape[1]
    return pl.pallas_call(
        rows_grad_kernel,
        grid=(width // 512,),
        in_specs=[pl.BlockSpec(left.shape, lambda t: (0, 0))]
        + [pl.BlockSpec((4 * ROWS, 512), lambda t: (0, t))] * 2,
        out_specs=pl.BlockSpec((left.shape[1], 512), lambda t: (0, t)),
        out_shape=jax.ShapeDtypeStruct((left.shape[1], width), BF),
        compiler_params=pltpu.CompilerParams(vmem_limit_bytes=LIMIT),
        cost_estimate=pl.CostEstimate(
            flops=10**9, bytes_accessed=6 * 10**6, transcendentals=0
        ),
        name="rows_grad",
    )(left, *rows)


def local_tokens(
    tokens,
    attn_norm,
    w_query,
    w_latent,
    latent_norm,
    w_expand,
    w_output,
    ffn_norm,
    w_router,
    shared_gate,
    shared_up,
    shared_down,
    expert_gate,
    expert_up,
    expert_down,
    out_grad,
    seq_length,
    expert_ids,
    fill_order,
):
    tok = tokens.shape[1]
    width = tokens.shape[2]
    n_dev = 32
    n_experts = 16
    n_blocks = n_dev
    capacity = tok * TOPK // n_experts
    pair_count = tok * TOPK
    my_y = lax.axis_index("y")
    my_x = lax.axis_index("x")
    my_c = lax.axis_index("c")
    my_z = lax.axis_index("z")
    own_tokens = tokens[0]
    input_rows = own_tokens.astype(F32)

    route_ids = expert_ids[0]
    flat_ids = route_ids.reshape(pair_count)
    ranks = slot_rank(flat_ids, fill_order[0]).reshape(tok, TOPK)
    kept = ranks < capacity
    same = route_ids[:, :, None] == jnp.arange(n_experts, dtype=jnp.int32)[None, None, :]
    slot_plus = jnp.sum(
        jnp.where(same & kept[:, :, None], ranks[:, :, None] + 1, 0), axis=1
    )
    slot_table = (slot_plus - 1).astype(BF)

    n_small = [tok, attn_norm.shape[0], ffn_norm.shape[0], latent_norm.shape[0], 16, w_router.size]
    small_all = jnp.concatenate(
        [
            attn_norm,
            ffn_norm,
            latent_norm,
            jnp.broadcast_to(seq_length.astype(BF), (16,)),
            w_router.reshape(-1),
        ]
    )
    to_each = jnp.concatenate(
        [
            jnp.concatenate([slot_table.T, slot_table.T], axis=0),
            jnp.broadcast_to(small_all[None], (n_dev, small_all.shape[0])),
        ],
        axis=1,
    )

    def column_tiles(value, groups):
        rows = value.shape[0]
        view = jnp.transpose(value.reshape(rows, -1, ROWS), (1, 0, 2))
        return view.reshape(groups, -1, ROWS)

    def natural_rows(value, rows):
        view = value.reshape(4, 2, 4, -1, rows, ROWS)
        view = jnp.transpose(view, (1, 0, 2, 4, 3, 5))
        return view.reshape(n_dev * rows, -1)

    query_rows = w_query.shape[0] * 3
    packed = jnp.concatenate([column_tiles(w_query, PAIRS), column_tiles(w_expand, PAIRS)], axis=1)
    wl_all = lax.all_gather(w_latent, ALL, axis=0, tiled=True)
    valid = (my_y * tok + jnp.arange(tok, dtype=jnp.int32) < seq_length[0]).astype(F32)
    grad_y = out_grad[0].astype(F32) * valid[:, None]
    grad_low = grad_y.astype(BF)
    n_shared = shared_down.shape[0]
    shared_pad = 128 - n_shared
    n_half = expert_down.shape[1]
    half_pad = -n_half % 256

    def widen_columns(value, amount):
        return jnp.pad(value, ((0, 0), (0, amount)))

    def halves(value):
        first, second = value[0, :, :n_half], value[0, :, n_half:]
        mine = jnp.where(my_y == 0, first, second)
        return mine, swap(jnp.where(my_y == 0, second, first), "y")

    def whole_rows(mine, other):
        both = jnp.concatenate(
            [jnp.where(my_y == 0, mine, other), jnp.where(my_y == 0, other, mine)], axis=0
        )
        return widen_columns(both, half_pad)

    def hidden_columns(value):
        return jnp.transpose(value.reshape(value.shape[0], n_dev, n_shared), (1, 0, 2))

    tokens_go = Chain(gather_hops(own_tokens))
    below_go = Chain(one_hop(shift_z(grad_low, 1)))
    packed = spread(packed, PLANE)
    packed, grad_low, w_output, expert_gate = tick(
        (packed, grad_low, w_output, expert_gate), tokens_go, below_go
    )
    packed_go = Chain(line_hops(packed))
    small = spread(to_each, ALL)
    grad_low = tick(grad_low, tokens_go, packed_go)
    grads_here = Chain(gather_hops(grad_low))
    small, grad_low, wl_all, expert_gate = tick(
        (small, grad_low, wl_all, expert_gate), tokens_go, packed_go, grads_here
    )
    tokens_here = tokens_go.result
    gate_mine, gate_go = halves(expert_gate)
    zq = swap_zq(w_output)
    latent_at = jnp.arange(KVR + 256)
    lane = (latent_at - KVR) % 128
    head = (latent_at - KVR) // 128
    latent_from = jnp.where(
        latent_at < KVR,
        latent_at,
        jnp.where(lane // 32 % 2 == head, KVR + lane % 32 + lane // 64 * 32, -1),
    )
    widen = (jnp.arange(KVR + ROPE)[:, None] == latent_from[None, :]).astype(BF)
    wl = matrix_product(wl_all, widen).astype(BF)
    grad_low, wl, gate_mine, zq = tick((grad_low, wl, gate_mine, zq), packed_go, grads_here)
    packed = packed_go.result
    below_go = Chain(gather_hops(below_go.result[0]))
    cuts = [sum(n_small[: i + 1]) for i in range(len(n_small))]
    slot_of = small[:, : cuts[0]].astype(F32)
    attention_gain = small[:, cuts[0] : cuts[1]].reshape(-1).astype(F32)
    feedforward_gain = small[:, cuts[1] : cuts[2]].reshape(-1).astype(F32)
    latent_gain = small[:, cuts[2] : cuts[3]].reshape(-1).astype(F32)
    lengths = small[:16, cuts[3]].astype(jnp.int32)
    router = small[:, cuts[4] : cuts[5]].reshape(width, n_experts)
    wq = natural_rows(packed[:, :, :query_rows], w_query.shape[0])
    we = natural_rows(packed[:, :, query_rows:], w_expand.shape[0])
    target = jnp.arange(384)
    rope_at = target - 256
    source = jnp.where(
        target < 256,
        target % 128 + target // 128 * 192,
        128 + rope_at % 32 + rope_at // 32 % 2 * 192 + rope_at // 64 * 32,
    )
    reorder = (jnp.arange(384)[:, None] == source[None, :]).astype(BF)
    wq = matrix_product(wq, reorder).astype(BF)
    half_pos = jnp.arange(tok, dtype=jnp.int32)
    pos_own = my_y * tok + half_pos
    cos_own, sin_own = rope_tables(pos_own, ROPE)
    cos_far, sin_far = rope_tables((1 - my_y) * tok + half_pos, ROPE)
    cos_pair = jnp.concatenate([jnp.concatenate([cos_own, cos_far], axis=0)] * 4, axis=1)
    sin_pair = jnp.concatenate([sin_own, sin_far], axis=0)
    sin_pair = jnp.concatenate([-sin_pair, -sin_pair, sin_pair, sin_pair], axis=1)
    my_seq = my_z * 4 + my_x * 2 + my_c
    meta = jnp.stack(
        [
            lengths[my_seq],
            lengths[my_z * 4 + (1 - my_x) * 2 + my_c],
            lengths[my_z * 4 + my_x * 2 + (1 - my_c)],
            lengths[my_z * 4 + (1 - my_x) * 2 + (1 - my_c)],
            my_y.astype(jnp.int32),
        ]
    )
    start = (wq, wl, we, meta, grad_low, zq, expert_up, shared_gate, shared_up)
    start = tick(start, grads_here, below_go)
    wq, wl, we, meta, grad_low, zq, expert_up, shared_gate, shared_up = start
    up_mine, up_go = halves(expert_up)

    wo = run(direct_hops(zq)).reshape(2 * VDIM, width)
    above_go = Chain(one_hop(shift_z(grad_low, -1)))
    kept_values = attend(
        meta, tokens_here, attention_gain, latent_gain, wq, wl, we, cos_pair, sin_pair
    )
    kept_values, up_mine, grad_low, gate_go = tick(
        (kept_values, up_mine, grad_low, gate_go), above_go, below_go
    )
    shared_both = spread(
        jnp.concatenate([hidden_columns(shared_gate), hidden_columns(shared_up)], axis=2), ALL
    )
    across_go = Chain(one_hop(shift_z(grad_low, 2)))
    above_go = Chain(gather_hops(above_go.result[0]))
    h_attn, query, latent, ropes, expand, attended, latent_raw = kept_values
    attended_parts = tick(project(attended, wo), above_go, below_go)
    grads_here = [grads_here.result, below_go.result]
    middle_go = Chain(reduce_hops(attended_parts))
    tick((), middle_go)
    up_go, shared_both = tick((up_go, shared_both), middle_go)
    tick((), middle_go, above_go, across_go)
    across_go = Chain(gather_hops(across_go.result[0]))
    middle = input_rows + middle_go.result

    h_ffn = rms_norm(middle, feedforward_gain).astype(BF)
    gates = jax.nn.softmax(matrix_product(h_ffn, router), axis=-1)
    gates_high = gates.astype(BF)
    gates_left = gates - gates_high.astype(F32)
    gates_middle = gates_left.astype(BF)
    gates_low = (gates_left - gates_middle.astype(F32)).astype(BF)
    gates_rest = jnp.zeros((tok, 128 - 3 * n_experts), BF)
    sent = jnp.concatenate([h_ffn, gates_high, gates_middle, gates_low, gates_rest], axis=1)

    sent = tick(sent, above_go, across_go)
    go = [Chain(gather_hops(sent))]
    below_go = Chain(one_hop(shift_z(sent, 1)))
    gate_w = whole_rows(gate_mine, gate_go)
    down_w = jnp.pad(expert_down[0], ((0, half_pad), (0, 0)))
    sent, gate_w, down_w = tick((sent, gate_w, down_w), go[0], below_go, across_go)
    across_sent = Chain(one_hop(shift_z(sent, 2)))
    go.append(Chain(gather_hops(below_go.result[0])))
    shared_both = shared_both.reshape(width, 2 * n_shared)
    shared_in = jnp.concatenate(
        [
            widen_columns(shared_both[:, :n_shared], shared_pad),
            widen_columns(shared_both[:, n_shared:], shared_pad),
        ],
        axis=1,
    )
    shared_out = jnp.pad(shared_down, ((0, shared_pad), (0, 0)))
    sent, shared_in, shared_out = tick(
        (sent, shared_in, shared_out), go[0], go[1], across_sent, across_go
    )
    above_sent = Chain(one_hop(shift_z(sent, -1)))
    go.append(Chain(gather_hops(across_sent.result[0])))
    weights = (gate_w, whole_rows(up_mine, up_go), down_w, shared_in, shared_out)
    weights = tick(weights, go[0], go[1], go[2], above_sent)
    go.append(Chain(gather_hops(above_sent.result[0])))
    grads_here.append(across_go.result)
    grads_here.append(above_go.result)

    plane = jnp.stack(
        [
            (my_y ^ dy) * 16 + (my_x ^ dx) * 2 + (my_c ^ dc)
            for dc in range(2)
            for dx in range(2)
            for dy in range(2)
        ]
    ).astype(jnp.int32)
    saved = []
    homes = []
    outs = []
    for number in range(4):
        index = plane + (my_z - STEPS[number]) % 4 * 4
        index = jnp.concatenate([index, my_seq[None].astype(jnp.int32)])
        results = ffn(
            index, go[number].result, grads_here[number], slot_of, weights, capacity
        )
        kept_here, d_h_parts, out_parts, weights = tick(
            results + (weights,), *go[number + 1 :], *homes, *outs[number // 3 :]
        )
        saved.append(kept_here)
        homes.append(Chain(home_hops(d_h_parts, STEPS[number])))
        outs.append(Chain(home_hops(out_parts, STEPS[number], ("y", "x"))))

    rows, grad_rows, act_weighted, d_gate_val, d_up_val = (
        jnp.concatenate([item[i] for item in saved], axis=0) for i in range(5)
    )

    def column_halves(left, right):
        value = dot_tn(left, right)[:, :n_half].astype(BF)
        first, second = value[: width // 2], value[width // 2 :]
        return jnp.where(my_y == 0, first, second), jnp.where(my_y == 0, second, first)

    def whole_columns(mine, other):
        return jnp.concatenate(
            [jnp.where(my_y == 0, mine, other), jnp.where(my_y == 0, other, mine)], axis=1
        ).astype(F32)

    rows, grad_rows = tick((rows, grad_rows), *homes, outs[3])
    d_gate_mine, d_gate_go = column_halves(rows, d_gate_val)
    rows, d_gate_mine, grad_rows = tick((rows, d_gate_mine, grad_rows), *homes)
    d_up_mine, d_up_go = column_halves(rows, d_up_val)
    d_up_mine, grad_rows = tick((d_up_mine, grad_rows), *homes, outs[1])
    grad_rows = tick(grad_rows, *homes, outs[0])
    d_h_ffn = add(*(home.result for home in homes))
    d_gates = d_h_ffn[:, width : width + n_experts] + d_h_ffn[:, width + 64 : width + 64 + n_experts]
    d_h_ffn = d_h_ffn[:, :width]

    d_logits = gates * (d_gates - jnp.sum(gates * d_gates, axis=-1, keepdims=True))
    d_h_ffn = d_h_ffn + jnp.dot(
        d_logits, router.astype(F32).T, precision=lax.Precision.HIGHEST
    )
    d_mid_norm, d_g_ffn = norm_back(middle, feedforward_gain, d_h_ffn)
    grad_mid = grad_y + d_mid_norm

    grad_mid = tick(grad_mid)
    douts_go = Chain(gather_hops(grad_mid.astype(BF)))
    d_down_w = dot_tn(act_weighted, grad_rows)[:n_half]
    d_down_w = tick(d_down_w, douts_go, outs[1])
    d_router = jnp.dot(h_ffn.astype(F32).T, d_logits, precision=lax.Precision.HIGHEST)
    d_router, d_gate_go = tick((d_router, d_gate_go), douts_go)
    d_gate_go = swap(d_gate_go, "y")
    d_gate_mine = tick(d_gate_mine, douts_go)
    d_wo = rows_grad(attended, douts_go.result)
    d_wo = tick(d_wo)
    wo_go = Chain(sum_hops(d_wo.reshape(4, -1, width), True))
    (d_query, d_expand), low_parts, hat_parts = tick(
        attend_back(
            meta, douts_go.result, query, ropes, expand, wq, we, wo, cos_pair, sin_pair
        ),
        wo_go,
        outs[2],
    )

    def by_owner(value, rows_each):
        view = value.astype(BF).reshape(2, 4, 4, rows_each, -1, ROWS)
        return jnp.transpose(view, (1, 0, 2, 4, 3, 5)).reshape(4, 8, -1, ROWS)

    low_go = Chain(reduce_hops(low_parts))
    hat_go = Chain(reduce_hops(hat_parts))
    d_query = dot_nt(d_query, reorder).astype(BF)
    d_packed = jnp.concatenate(
        [
            by_owner(dot_tn(h_attn, d_query), w_query.shape[0]),
            by_owner(dot_tn(latent, d_expand), w_expand.shape[0]),
        ],
        axis=2,
    )
    d_packed, shared_sums, d_gate_go, d_up_go = tick(
        (d_packed, [item[5:7] for item in saved], d_gate_go, d_up_go), low_go, hat_go, outs[2]
    )
    d_up_go = swap(d_up_go, "y")
    d_packed = run(sum_hops(d_packed, True))
    d_shared_in = sum(item[0] for item in shared_sums).astype(BF).T
    d_shared_in = d_shared_in.reshape(n_dev, width // n_dev, 256)
    d_shared_in = jnp.concatenate(
        [d_shared_in[..., :n_shared], d_shared_in[..., 128 : 128 + n_shared]], axis=2
    )
    d_shared_in, d_up_go = tick((d_shared_in, d_up_go), low_go, hat_go)
    d_shared_down = sum(item[1] for item in shared_sums)[:n_shared]
    d_shared_down = tick(d_shared_down, low_go, hat_go, outs[3])
    d_low = low_go.result
    d_latent_raw, d_g_latent = norm_back(latent_raw, latent_gain, d_low[:, :KVR])
    d_rope = jnp.concatenate([d_low[:, KVR : KVR + 32], d_low[:, KVR + 64 : KVR + 96]], axis=1)
    d_rope_raw = rotate_back(d_rope, cos_own, sin_own)
    d_latent_in = jnp.concatenate([d_latent_raw, d_rope_raw], axis=-1).astype(BF)
    dlat_here = run(gather_hops(d_latent_in))
    d_hattn = hat_go.result + dot_nt(d_latent_in, wl_all)
    d_in_norm, d_g_attn = norm_back(input_rows, attention_gain, d_hattn)
    input_grad = (grad_mid + d_in_norm).astype(BF)
    early = jnp.concatenate([d_g_ffn.reshape(n_dev, -1), d_router.reshape(n_dev, -1)], axis=1)
    small_grads = jnp.concatenate(
        [early, d_g_attn.reshape(n_dev, -1), d_g_latent.reshape(n_dev, -1)], axis=1
    )
    small_grads = spread(small_grads, ALL)
    wo_back = swap_zq(wo_go.result)
    my_pair = my_y * 4 + my_x * 2 + my_c
    part_cols = w_latent.shape[1] // PAIRS
    plane_dlat = jnp.concatenate(dlat_here, axis=0)
    d_columns = lax.dynamic_slice_in_dim(
        widen_columns(plane_dlat, 64), my_pair * part_cols, ROWS, axis=1
    )
    latent_go = Chain(sum_hops(by_owner(dot_tn(h_attn, d_columns), w_latent.shape[0]), True))
    d_packed = tick(d_packed, latent_go, outs[2], outs[3])
    d_packed = spread(
        jnp.concatenate([d_packed, latent_go.result], axis=1), PLANE
    ).astype(F32)
    split = w_query.shape[0] * 3
    wq_grad = jnp.transpose(
        d_packed[:, :split].reshape(PAIRS, 3, w_query.shape[0], ROWS), (2, 0, 1, 3)
    ).reshape(w_query.shape)
    we_grad = jnp.transpose(
        d_packed[:, split : -w_latent.shape[0]].reshape(PAIRS, 4, w_expand.shape[0], ROWS),
        (2, 0, 1, 3),
    ).reshape(w_expand.shape)
    wl_grad = jnp.transpose(
        d_packed[:, -w_latent.shape[0] :, :part_cols], (1, 0, 2)
    ).reshape(w_latent.shape)
    wo_grad = wo_back.astype(F32)
    d_shared_in = spread(d_shared_in, ALL).astype(F32)

    def shared_columns(value):
        return jnp.transpose(value, (1, 0, 2)).reshape(width // n_dev, n_dev * n_shared)

    d_shared_gate = shared_columns(d_shared_in[..., :n_shared])
    d_shared_up = shared_columns(d_shared_in[..., n_shared:])
    d_expert_gate = whole_columns(d_gate_mine, d_gate_go)
    d_expert_up = whole_columns(d_up_mine, d_up_go)
    output = add(middle, *(finish(out) for out in outs)).astype(BF)
    small_grads = jnp.sum(small_grads, axis=0)
    rows_each = width // n_dev
    gffn_grad = small_grads[:rows_each]
    router_grad = small_grads[rows_each : rows_each * (1 + n_experts)].reshape(rows_each, n_experts)
    late = small_grads[rows_each * (1 + n_experts) :]
    return (
        output[None],
        input_grad[None],
        late[: width // n_dev],
        wq_grad,
        wl_grad,
        late[width // n_dev :],
        we_grad,
        wo_grad,
        gffn_grad,
        router_grad,
        d_shared_gate,
        d_shared_up,
        d_shared_down,
        d_expert_gate[None],
        d_expert_up[None],
        d_down_w[None],
    )


def tokens_plan(mesh):
    fine = Mesh(mesh.devices.reshape(2, 4, 2, 2), ALL)
    rows = P(FSDP, "y", None)
    vector = P(ALL)
    matrix = P(ALL, None)
    in_specs = (
        rows,
        vector,
        matrix,
        matrix,
        vector,
        matrix,
        matrix,
        vector,
        matrix,
        matrix,
        matrix,
        matrix,
        rows,
        rows,
        rows,
        rows,
        P(FSDP),
        rows,
        P(FSDP, "y"),
    )
    out_specs = (
        rows,
        rows,
        vector,
        matrix,
        matrix,
        vector,
        matrix,
        matrix,
        vector,
        matrix,
        matrix,
        matrix,
        matrix,
        rows,
        rows,
        rows,
    )
    return jax.shard_map(
        local_tokens, mesh=fine, in_specs=in_specs, out_specs=out_specs, check_vma=False
    )


def weights_plan(mesh):
    in_specs = (
        P("fsdp", "ctx", None),
        P(("ctx", "fsdp")),
        P(("ctx", "fsdp"), None),
        P(("ctx", "fsdp"), None),
        P(("ctx", "fsdp")),
        P(("ctx", "fsdp"), None),
        P(("ctx", "fsdp"), None),
        P(("ctx", "fsdp")),
        P(("ctx", "fsdp"), None),
        P(("ctx", "fsdp"), None),
        P(("ctx", "fsdp"), None),
        P(("ctx", "fsdp"), None),
        P("fsdp", "ctx", None),
        P("fsdp", "ctx", None),
        P("fsdp", "ctx", None),
        P("fsdp", "ctx", None),
        P("fsdp"),
        P("fsdp", "ctx", None),
        P("fsdp", "ctx"),
    )
    out_specs = (
        P("fsdp", "ctx", None),
        P("fsdp", "ctx", None),
        P(("ctx", "fsdp")),
        P(("ctx", "fsdp"), None),
        P(("ctx", "fsdp"), None),
        P(("ctx", "fsdp")),
        P(("ctx", "fsdp"), None),
        P(("ctx", "fsdp"), None),
        P(("ctx", "fsdp")),
        P(("ctx", "fsdp"), None),
        P(("ctx", "fsdp"), None),
        P(("ctx", "fsdp"), None),
        P(("ctx", "fsdp"), None),
        P("fsdp", "ctx", None),
        P("fsdp", "ctx", None),
        P("fsdp", "ctx", None),
    )
    return jax.shard_map(local_weights, mesh=mesh, in_specs=in_specs, out_specs=out_specs, check_vma=False)


def solution(mesh):
    if mesh.shape["ctx"] == 2 and mesh.shape["fsdp"] == 16:
        return tokens_plan(mesh)
    return weights_plan(mesh)
```
